128 devices in a mesh: section: 8 (over y, z_lo), dp: 16 (over z_hi, x, core).
Axes of the slice: x: 4, y: 4, z: 4 (z_hi: 2, z_lo: 2; z = z_hi * 2 + z_lo), core: 2. Of those that a mesh axis runs over, the one named last changes fastest.
Arguments:
- embedded: bfloat16 [8192, 1536], P('dp'), may hold values from -6 to 6
- hidden_out: bfloat16 [8, 8192, 1536], P('section', 'dp'), may hold values from -6 to 6
- out_grads: bfloat16 [8, 8192, 8192], P('section', 'dp'), may hold values from -6 to 6
- counts: int32 [16, 2], replicated, may hold values from 64 to 256, as said below
- owners: int32 [8, 12, 1], P('section'), may hold values from 0 to 15; in each aligned block of 12 rows (0 to 11, 12 to 23, ..., all dimensions but the last counted through in order) at most 2 rows name the same one
- ginv: bfloat16 [8, 64, 128, 128], P('section', 'dp'), as said below
- ainv: bfloat16 [8, 16, 2, 128, 128], P('section', 'dp'), as said below
Outputs:
- update: bfloat16 [8, 8192, 1536], P('section', 'dp')
The draws below stay inside these ranges and needn't reach their ends.
Inputs may be any that keep to these rules, and one draw needn't show every extreme that they name: `counts`: every replica fills its slots from the front; in every draw some micro-batch is full with 256 valid tokens. `owners`: within one layer no replica holds more than 2 tiles, and in every draw some replica holds exactly 2 tiles of some layer. `ginv`: symmetric blocks. `ainv`: symmetric blocks; slots that no tile uses hold arbitrary values.
All inputs are finite; a program needn't handle non-finite values.
Results may differ from the reference program's by a relative error of at most 0.022.
Values may be sent and summed in bfloat16 or wider, within the bound.
A program may use at most 192 MiB of HBM per device.

```python
import math
import jax
import jax.numpy as jnp
import numpy as np
from jax import lax

D = 8192
BLOCK = 128
TILES = 12
CAP = 2
MICRO = 2
MB_ROWS = 256
WINDOW = 1536
GBLOCKS = 64
LAYERS = 8
REPLICAS = 16
TOKENS = 8192


def factor_matrices(key, shape, block_size, low, high):
    key_noise, key_diag = jax.random.split(key)
    noise = jax.random.normal(key_noise, shape, jnp.float32)
    symmetric = (noise + jnp.swapaxes(noise, -1, -2)) * (0.35 / math.sqrt(block_size))
    diagonal = jax.random.uniform(key_diag, shape[:-1], jnp.float32, low, high)
    return symmetric + diagonal[..., None] * jnp.eye(block_size, dtype=jnp.float32)


def draw_ainv(key, part):
    key = jax.random.fold_in(key, 11)
    low, high = (1.0, 2.0)
    return factor_matrices(key, (LAYERS, REPLICAS, CAP, BLOCK, BLOCK), BLOCK, low, high).astype(jnp.bfloat16)


def draw_ginv(key, part):
    key = jax.random.fold_in(key, 23)
    low, high = (1.0, 2.0)
    return factor_matrices(key, (LAYERS, GBLOCKS, BLOCK, BLOCK), BLOCK, low, high).astype(jnp.bfloat16)


def draw_counts(key, part):
    key = jax.random.fold_in(key, 37)
    key_values, key_full = jax.random.split(key)
    total_slots = REPLICAS * MICRO
    values = jax.random.randint(key_values, (total_slots,), MB_ROWS // 4, MB_ROWS + 1)
    full_slot = jax.random.randint(key_full, (), 0, total_slots)
    values = jnp.where(jnp.arange(total_slots) == full_slot, MB_ROWS, values)
    return values.reshape(REPLICAS, MICRO).astype(jnp.int32)


def with_spikes(values, own_key, source, target, parts, factor):
    owner, partner = [(jnp.arange(values.shape[axis_at]) // (values.shape[axis_at] // parts)).reshape([-1 if axis == axis_at else 1 for axis in range(values.ndim)]) for axis_at in (source, target)]
    chosen = jax.random.permutation(own_key, parts)[partner]
    strong = (owner == chosen) | (owner == (partner + parts // 2) % parts)
    return jnp.where(strong, factor * values, values)


def levels(own_key, extent, cuts, low, high):
    loudness = 1.0
    for position, blocks in cuts:
        steps = jax.random.uniform(jax.random.fold_in(jax.random.fold_in(own_key, 6), position), (blocks,), jnp.float32, low / len(cuts), high / len(cuts))
        loudness = loudness * jnp.repeat(jnp.exp(steps), extent[position] // blocks).reshape((-1,) + (1,) * (len(extent) - 1 - position))
    return loudness


def routed_block(rng, own, number, rows, count, top, bound, slope):
    ranking = jax.random.permutation(rng, count)
    crowded, common = load_shares(count, rows * top, bound, slope, True), load_shares(count, rows * top, bound, slope, False)
    places = jnp.arange(count)

    def named(tallies, rotation):
        used = int((tallies > 0).sum())
        fixed = max(1, used // 4)
        passed = fixed + (places - fixed + rotation * (used - fixed)) % max(1, count - fixed)
        return jnp.zeros((count,), jnp.int32).at[ranking[jnp.where(places < fixed, places, passed)]].set(jnp.asarray(tallies, jnp.int32))

    tallies = jnp.where(number % 4 == 0, named(crowded, number // 4), named(common, number - number // 4 - 1))
    mixed = jax.random.permutation(jax.random.fold_in(own, 3), count)
    donor, sink = mixed[0:count // 2 * 2:2], mixed[1:count // 2 * 2:2]
    margin = jnp.minimum(tallies[donor] - 1, bound - tallies[sink]) // 2
    margin = jnp.where((donor == ranking[0]) | (sink == ranking[0]) | (tallies[sink] == 0), 0, jnp.maximum(margin, 0))
    passed = jax.random.randint(jax.random.fold_in(own, 4), (count // 2,), 0, 1 << 20) % (margin + 1)
    tallies = tallies.at[donor].add(-passed).at[sink].add(passed)
    items = jnp.searchsorted(jnp.cumsum(tallies), jnp.arange(rows * top), side="right").astype(jnp.int32)
    listing = items.reshape(top, rows).T
    listing = listing[jax.random.permutation(jax.random.fold_in(own, 1), rows)]
    rotation = jax.random.randint(jax.random.fold_in(own, 2), (rows, 1), 0, top)
    return jnp.take_along_axis(listing, (jnp.arange(top)[None, :] + rotation) % top, axis=1)


def load_shares(number_of, total, reach, lean, full):
    loads = [(1 << 20) // math.isqrt(standing ** lean) + 1 for standing in range(1, number_of + 1)]
    largest = reach if full else min(reach, max(-(-total // number_of), total * loads[0] // sum(loads)))
    least = 1 if total - largest >= number_of - 1 else 0
    given, rest = [largest] + [least] * (number_of - 1), total - largest - least * (number_of - 1)
    while rest > 0:
        movable = [i for i in range(1, number_of) if given[i] < largest] or [i for i in range(1, number_of) if given[i] < reach]
        mass, budget = sum([loads[i] for i in movable]), rest
        for i in movable:
            more = min(reach - given[i], max(1, budget * loads[i] // mass), rest)
            given[i] = given[i] + more
            rest = rest - more
    return np.array(given)


def normal_values(stream_key, shape, width, most, shards=(), held_as=jnp.bfloat16):
    level = levels(stream_key, shape, shards, -0.22, 0.18) if shards else 1.0
    drawn = jax.random.normal(stream_key, shape, jnp.float32) * width * level
    return jnp.minimum(jnp.maximum(drawn, -most), most).astype(held_as)


def bell_draw_with(rng, dims, spread, most, cuts, heavy, kind=jnp.bfloat16):
    values = spread * jax.random.normal(rng, dims, jnp.float32)
    if cuts:
        values = values * levels(rng, dims, cuts, -0.22, 0.18)
    return jnp.clip(with_spikes(values, jax.random.fold_in(rng, 3), *heavy), -most, most).astype(kind)


def setup_inputs(seed: int = 0) -> dict:
    keys = jax.random.split(jax.random.key(seed), 8)
    embedded = normal_values(keys[0], (TOKENS, WINDOW), 1.0, 6.0, ((0, 16),))
    hidden_out = normal_values(keys[1], (LAYERS, TOKENS, WINDOW), 1.0, 6.0, ((0, 8), (1, 16)))
    out_grads = bell_draw_with(keys[2], (LAYERS, TOKENS, D), 1.0, 6.0, ((0, 8), (1, 16)), (1, 2, 16, 2.0))
    counts = draw_counts(jax.random.fold_in(keys[7], 71), 0)
    owners_keys = jax.random.split(jax.random.fold_in(keys[4], 1), LAYERS * TILES // TILES)
    owners_turns = jax.random.permutation(jax.random.fold_in(keys[4], 3), LAYERS * TILES // TILES)
    owners = jax.vmap(lambda own, number: routed_block(jax.random.fold_in(keys[4], 2), own, number, TILES, REPLICAS, 1, CAP, 2))(owners_keys, owners_turns).reshape((LAYERS, TILES, 1))
    ginv = draw_ginv(jax.random.fold_in(keys[7], 71), 0)
    ainv = draw_ainv(jax.random.fold_in(keys[7], 71), 0)
    return dict(embedded=embedded, hidden_out=hidden_out, out_grads=out_grads, counts=counts, owners=owners, ginv=ginv, ainv=ainv)


def slots_of(owner_ids):
    shared = owner_ids[:, None, :] == owner_ids[:, :, None]
    tile_index = jnp.arange(TILES)
    earlier = tile_index[None, :] < tile_index[:, None]
    return lax.optimization_barrier(jnp.sum(shared & earlier[None], axis=2)).astype(jnp.int32)

def reference(embedded, hidden_out, out_grads, counts, owners, ginv, ainv):
    inputs = jnp.concatenate([embedded[None], hidden_out[:-1]], axis=0)
    positions = jnp.arange(MB_ROWS)
    usable = (positions[None, None, :] < counts[:, :, None]).reshape(REPLICAS * MICRO * MB_ROWS)
    token_scale = 1.0 / jnp.sqrt(jnp.sum(counts).astype(jnp.float32))
    owner_ids = owners[:, :, 0]
    slot_ids = slots_of(owner_ids)
    rows_dev = MICRO * MB_ROWS

    def one_layer(operands):
        layer_in, layer_grad, gain_blocks, factor_slots, owner_row, slot_row = operands
        masked = layer_grad * usable[:, None].astype(jnp.bfloat16)
        grad_parts = masked.reshape(REPLICAS, rows_dev, D)
        input_parts = layer_in.reshape(REPLICAS, rows_dev, WINDOW)

        def add_replica(running, pieces):
            partial_value = lax.dot_general(pieces[0], pieces[1], (((0,), (0,)), ((), ())), preferred_element_type=jnp.float32) * token_scale
            rounded = lax.optimization_barrier(partial_value.astype(jnp.bfloat16))
            return (running + rounded.astype(jnp.float32), None)
        grad, _ = lax.scan(add_replica, jnp.zeros((D, WINDOW), jnp.float32), (grad_parts, input_parts))
        gradb = grad.astype(jnp.bfloat16)
        adjusted = jnp.einsum('bij,bjw->biw', gain_blocks.astype(jnp.float32), gradb.reshape(GBLOCKS, BLOCK, WINDOW).astype(jnp.float32))
        adjusted = adjusted.reshape(D, WINDOW).astype(jnp.bfloat16)
        chosen = factor_slots[owner_row, slot_row]
        result = jnp.einsum('rtk,tkj->rtj', adjusted.reshape(D, TILES, BLOCK).astype(jnp.float32), chosen.astype(jnp.float32))
        return result.reshape(D, WINDOW).astype(jnp.bfloat16)
    return lax.map(one_layer, (inputs, out_grads, ginv, ainv, owner_ids, slot_ids))
```

```python
import functools

import jax
import jax.numpy as jnp
from jax import lax
from jax.experimental import pallas as pl
from jax.experimental.pallas import tpu as pltpu
from jax.sharding import PartitionSpec as P

MESH = pl.DeviceIdType.MESH
F32 = jnp.float32
BF16 = jnp.bfloat16

CW = 128
AHEAD = 4


def kernel(
    dims, emb, hid, og, counts, owners, ginv, ainv, out,
    a_buf, b_buf, bt, m1, r1, m2, r2, own, zs, zr, ag, obuf,
    a_loc, a_snd, a_rcv, b_snd, b_rcv, f_snd, f_rcv, m1_snd, m1_rcv, m2_snd, m2_rcv,
    z_snd, z_rcv, g_snd, g_rcv, o_sem,
):
    sections, nx, rows, tok, window = dims
    nc = window // CW
    s = lax.axis_index("section")
    dp = lax.axis_index("dp")
    zh, x, c = dp // (2 * nx), (dp // 2) % nx, dp % 2

    def at(dx=0, z=None, core=None):
        z = zh if z is None else z
        core = c if core is None else core
        return (s, (z * nx + (x + dx) % nx) * 2 + core)

    right, left, across = at(1), at(nx - 1), at(2)
    opposite, partner = at(z=1 - zh), at(core=1 - c)
    following, previous = ((s + 1) % sections, dp), ((s + sections - 1) % sections, dp)

    def remote(src, dst, snd, rcv, device):
        return pltpu.make_async_remote_copy(
            src_ref=src, dst_ref=dst, send_sem=snd, recv_sem=rcv,
            device_id=device, device_id_type=MESH,
        )

    def columns_of(z, dx, core):
        block = (z * nx + (x + dx) % nx) * 2 + core
        return pl.ds(pl.multiple_of(block * rows, rows), rows)

    def a_local(z, dx):
        q = z * nx + dx
        return pltpu.make_async_copy(
            og.at[0, :, columns_of(z, dx, c)], a_buf.at[q, pl.ds(0, tok), :], a_loc.at[q]
        )

    def a_remote(z, dx):
        q = z * nx + dx
        return remote(
            og.at[0, :, columns_of(z, dx, 1 - c)], a_buf.at[q, pl.ds(tok, tok), :],
            a_snd.at[q], a_rcv.at[q], partner,
        )

    def window_cols(j):
        return pl.ds(pl.multiple_of(j * CW, CW), CW)

    def b_local(j):
        return pltpu.make_async_copy(
            emb.at[:, window_cols(j)], b_buf.at[j, pl.ds(0, tok), :], b_rcv.at[j]
        )

    def b_remote(j):
        return remote(
            hid.at[0, :, window_cols(j)], b_buf.at[j, pl.ds(0, tok), :],
            b_snd.at[j], b_rcv.at[j], following,
        )

    def forward(j):
        return remote(
            b_buf.at[j, pl.ds(0, tok), :], b_buf.at[j, pl.ds(tok, tok), :],
            f_snd.at[j], f_rcv.at[j], partner,
        )

    def first(d, j):
        return remote(
            m1.at[d, j], r1.at[d, j], m1_snd.at[d, j], m1_rcv.at[d, j], left if d else right
        )

    def second(d, z, j):
        return remote(
            m2.at[d, z, j], r2.at[d, z, j], m2_snd.at[d, z, j], m2_rcv.at[d, z, j],
            left if d else right,
        )

    def last(j):
        return remote(zs.at[j], zr.at[j], z_snd.at[j], z_rcv.at[j], opposite)

    def factor_x(k):
        return remote(
            ag.at[c, zh, x], ag.at[c, zh, x], g_snd.at[k - 1], g_rcv.at[k - 1], at(k)
        )

    def factor_z():
        return remote(ag.at[c, zh], ag.at[c, zh], g_snd.at[3], g_rcv.at[3], opposite)

    def factor_c():
        return remote(ag.at[c], ag.at[c], g_snd.at[4], g_rcv.at[4], partner)

    def store(j):
        return pltpu.make_async_copy(obuf.at[j], out.at[0, :, window_cols(j)], o_sem.at[j])

    def send_b(j):
        @pl.when(s == 0)
        def _():
            b_local(j).start()

        @pl.when(s < sections - 1)
        def _():
            b_remote(j).start()

    def take_b(j):
        @pl.when(s == 0)
        def _():
            b_local(j).wait()

        @pl.when(s > 0)
        def _():
            b_remote(j).wait_recv()

        forward(j).start()

    def wait_a(*pairs):
        for z, dx in pairs:
            a_local(z, dx).wait()
            a_remote(z, dx).wait_recv()

    for z, dx in ((0, 2), (1, 2), (1, 1), (0, 3), (0, 1), (1, 3), (0, 0), (1, 0)):
        a_local(z, dx).start()
    barrier = pltpu.get_barrier_semaphore()
    neighbours = (right, left, across, opposite, partner, following, previous)
    for device in neighbours:
        pl.semaphore_signal(barrier, inc=1, device_id=device, device_id_type=MESH)
    ag[c, zh, x] = ainv[0, 0]
    pl.semaphore_wait(barrier, len(neighbours))

    send_b(0)
    for z, dx in ((0, 2), (1, 2), (1, 1), (0, 3), (0, 1), (1, 3)):
        a_remote(z, dx).start()
    for j in range(1, min(AHEAD, nc)):
        send_b(j)
    for k in range(1, nx):
        factor_x(k).start()
    take_b(0)
    for z, dx in ((0, 0), (1, 0)):
        a_remote(z, dx).start()

    def bounds(core):
        replica = (zh * nx + x) * 2 + core
        return counts[replica, 0], counts[replica, 1]

    limits = (*bounds(c), *bounds(1 - c))
    half = tok // 2

    def transpose_b(j):
        for p in range(4):
            piece = b_buf[j, pl.ds(p * half, half), :].astype(F32)
            slots = lax.broadcasted_iota(jnp.int32, piece.shape, 0)
            piece = jnp.where(slots < limits[p], piece, 0.0)
            bt[j, :, pl.ds(p * half, half)] = piece.T.astype(BF16)

    def term(j, q):
        return jnp.dot(bt[j], a_buf[q], preferred_element_type=F32)

    def finish(j):
        total = jnp.int32(0)
        for r in range(counts.shape[0]):
            for m in range(counts.shape[1]):
                total = total + counts[r, m]
        scale = 1.0 / jnp.sqrt(jnp.full((1, rows), total.astype(F32)))
        grad = ((own[j % 2] + zr[j].astype(F32)) * scale).astype(BF16)
        blocks = ginv.shape[1]
        size = ginv.shape[-1]
        adjusted = jnp.concatenate(
            [
                jnp.dot(grad[:, b * size:(b + 1) * size], ginv[0, b], preferred_element_type=F32)
                for b in range(blocks)
            ],
            axis=1,
        ).astype(BF16)
        for k in range(CW // size):
            t = j * (CW // size) + k
            owner = owners[0, t, 0]
            slot = jnp.int32(0)
            for t2 in range(window // size):
                slot = slot + jnp.where((owners[0, t2, 0] == owner) & (t2 < t), 1, 0)
            slot = jnp.minimum(slot, ainv.shape[2] - 1)
            factor = ag[owner % 2, owner // (2 * nx), (owner // 2) % nx, slot]
            piece = jnp.dot(
                factor, adjusted[k * size:(k + 1) * size, :], preferred_element_type=F32
            )
            obuf[j, :, pl.ds(k * size, size)] = piece.T.astype(BF16)
        store(j).start()

    def step(i, carry):
        @pl.when((i >= 2) & (i < nc + 2))
        def _():
            j = i - 2

            @pl.when(i == 2)
            def _():
                wait_a((0, 1), (1, 3))

            for d, q in ((0, 1), (1, nx + 3)):
                value = term(j, q)
                first(d, j).wait_recv()
                m2[d, d, j] = (value + r1[d, j].astype(F32)).astype(BF16)
                second(d, d, j).start()

        @pl.when(i < nc)
        def _():
            @pl.when(i == 0)
            def _():
                wait_a((0, 2), (1, 2))

            forward(i).wait_recv()
            transpose_b(i)
            for d, q in ((0, 2), (1, nx + 2)):
                m1[d, i] = term(i, q).astype(BF16)
                first(d, i).start()

        @pl.when((i >= 1) & (i < nc + 1))
        def _():
            @pl.when(i == 1)
            def _():
                wait_a((1, 1), (0, 3))

            j = i - 1
            for d, q in ((0, nx + 1), (1, 3)):
                m2[d, 1 - d, j] = term(j, q).astype(BF16)
                second(d, 1 - d, j).start()

        @pl.when(i + AHEAD < nc)
        def _():
            send_b(i + AHEAD)

        @pl.when(i + 1 < nc)
        def _():
            take_b(i + 1)

        @pl.when(i == 1)
        def _():
            for k in range(1, nx):
                factor_x(k).wait_recv()
            factor_z().start()

        @pl.when(i == 2)
        def _():
            factor_z().wait_recv()
            factor_c().start()

        @pl.when((i >= 2) & (i < nc + 2))
        def _():
            j = i - 2

            @pl.when(i == 2)
            def _():
                wait_a((0, 0), (1, 0))

            away = term(j, (1 - zh) * nx)
            mine = term(j, zh * nx)
            second(0, 1, j).wait_recv()
            second(1, 0, j).wait_recv()
            second(0, 0, j).wait_recv()
            second(1, 1, j).wait_recv()
            zs[j] = (
                away + r2[0, 1 - zh, j].astype(F32) + r2[1, 1 - zh, j].astype(F32)
            ).astype(BF16)
            last(j).start()
            own[j % 2] = mine + r2[0, zh, j].astype(F32) + r2[1, zh, j].astype(F32)

        @pl.when(i >= 3)
        def _():
            @pl.when(i == 3)
            def _():
                factor_c().wait_recv()

            last(i - 3).wait_recv()
            finish(i - 3)

        return carry

    lax.fori_loop(0, nc + 3, step, 0)

    for z in range(2):
        for dx in range(nx):
            a_remote(z, dx).wait_send()
    for k in range(1, nx):
        factor_x(k).wait_send()
    factor_z().wait_send()
    factor_c().wait_send()

    def drain(j, carry):
        @pl.when(s < sections - 1)
        def _():
            b_remote(j).wait_send()

        forward(j).wait_send()
        for d in range(2):
            first(d, j).wait_send()
            for z in range(2):
                second(d, z, j).wait_send()
        last(j).wait_send()
        store(j).wait()
        return carry

    lax.fori_loop(0, nc, drain, 0)


def local(sections, groups, embedded, hidden_out, out_grads, counts, owners, ginv, ainv):
    tok, window = embedded.shape
    rows = out_grads.shape[-1] // groups
    nx = groups // 4
    nc = window // CW
    dims = (sections, nx, rows, tok, window)
    hbm = pl.BlockSpec(memory_space=pl.ANY)
    vmem = pl.BlockSpec(memory_space=pltpu.VMEM)
    smem = pl.BlockSpec(memory_space=pltpu.SMEM)
    dma = pltpu.SemaphoreType.DMA
    flops = 2 * tok * out_grads.shape[-1] * window
    return pl.pallas_call(
        functools.partial(kernel, dims),
        out_shape=jax.ShapeDtypeStruct((1, rows, window), BF16),
        in_specs=[hbm, hbm, hbm, smem, smem, vmem, vmem],
        out_specs=hbm,
        scratch_shapes=[
            pltpu.VMEM((2 * nx, 2 * tok, rows), BF16),
            pltpu.VMEM((nc, 2 * tok, CW), BF16),
            pltpu.VMEM((nc, CW, 2 * tok), BF16),
            pltpu.VMEM((2, nc, CW, rows), BF16),
            pltpu.VMEM((2, nc, CW, rows), BF16),
            pltpu.VMEM((2, 2, nc, CW, rows), BF16),
            pltpu.VMEM((2, 2, nc, CW, rows), BF16),
            pltpu.VMEM((2, CW, rows), F32),
            pltpu.VMEM((nc, CW, rows), BF16),
            pltpu.VMEM((nc, CW, rows), BF16),
            pltpu.VMEM((2, 2, nx) + ainv.shape[2:], BF16),
            pltpu.VMEM((nc, rows, CW), BF16),
            dma((2 * nx,)), dma((2 * nx,)), dma((2 * nx,)),
            dma((nc,)), dma((nc,)), dma((nc,)), dma((nc,)),
            dma((2, nc)), dma((2, nc)), dma((2, 2, nc)), dma((2, 2, nc)),
            dma((nc,)), dma((nc,)), dma((nx + 1,)), dma((nx + 1,)), dma((nc,)),
        ],
        compiler_params=pltpu.CompilerParams(
            collective_id=0, has_side_effects=True, vmem_limit_bytes=56 << 20
        ),
        cost_estimate=pl.CostEstimate(
            flops=flops, bytes_accessed=2 * out_grads.size, transcendentals=0
        ),
    )(embedded, hidden_out, out_grads, counts, owners, ginv, ainv)


def solution(mesh):
    placed = (
        P("dp", None),
        P("section", "dp", None),
        P("section", "dp", None),
        P(),
        P("section", None, None),
        P("section", "dp", None, None),
        P("section", "dp", None, None, None),
    )
    return jax.shard_map(
        functools.partial(local, mesh.shape["section"], mesh.shape["dp"]),
        mesh=mesh, in_specs=placed, out_specs=P("section", "dp", None), check_vma=False,
    )
```

```python
import functools

import jax
import jax.numpy as jnp
from jax import lax
from jax.experimental import pallas as pl
from jax.experimental.pallas import tpu as pltpu
from jax.sharding import PartitionSpec as P

MESH = pl.DeviceIdType.MESH
F32 = jnp.float32
BF16 = jnp.bfloat16

SW = 128
SUBS = 2
CW = SUBS * SW
UW = 512
AHEAD = 4
LAG = 2
PACE = (2, 2, 1, 1, 1, 1)


def kernel(
    dims, emb, hid, og, counts_in, owners_in, ginv, ainv, out,
    counts, owners, a_buf, a2, b_buf, b2, bt, bt2, m1, r1, m2, r2, own, zs, zr,
    n1, s1, n2, s2, comb, own2, ag, chosen, obuf, obuf2, hbuf, tbuf,
    i_sem, l_sem, t_sem, a_loc, a_snd, a_rcv, c_loc, c_snd, c_rcv, b_snd, b_rcv, e_snd, e_rcv, f_snd, f_rcv,
    h_snd, h_rcv, m1_snd, m1_rcv, m2_snd, m2_rcv, n1_snd, n1_rcv, n2_snd, n2_rcv,
    z_snd, z_rcv, g_snd, g_rcv, o_sem, o2_sem,
):
    sections, nx, rows, tok, window = dims
    nc = window // CW
    ns = window // SW
    nu = window // UW
    uw = UW
    size = ginv.shape[-1]
    blocks = ginv.shape[1]
    tail = size
    main = rows - tail
    s = lax.axis_index("section")
    dp = lax.axis_index("dp")
    zh, x, c = dp // (2 * nx), (dp // 2) % nx, dp % 2

    def spot(dx=0, z=None, core=None):
        z = zh if z is None else z
        core = c if core is None else core
        return (z * nx + (x + dx) % nx) * 2 + core

    right, left, across = (s, spot(1)), (s, spot(nx - 1)), (s, spot(2))
    opposite, partner = (s, spot(z=1 - zh)), (s, spot(core=1 - c))
    diagonal = (s, spot(z=1 - zh, core=1 - c))
    following, previous = ((s + 1) % sections, dp), ((s + sections - 1) % sections, dp)
    following2, previous2 = (following[0], opposite[1]), (previous[0], opposite[1])

    def remote(src, dst, snd, rcv, device):
        return pltpu.make_async_remote_copy(
            src_ref=src, dst_ref=dst, send_sem=snd, recv_sem=rcv,
            device_id=device, device_id_type=MESH,
        )

    def main_of(z, dx, core):
        return pl.ds(pl.multiple_of(spot(dx, z, core) * rows, rows), main)

    def tail_of(z, dx, core):
        return pl.ds(pl.multiple_of(spot(dx, z, core) * rows + main, tail), tail)

    def a_local(z, dx):
        q = z * nx + dx
        return pltpu.make_async_copy(
            og.at[0, :, main_of(z, dx, c)], a_buf.at[q, pl.ds(0, tok), :], a_loc.at[q]
        )

    def a_remote(z, dx):
        q = z * nx + dx
        return remote(
            og.at[0, :, main_of(z, dx, 1 - c)], a_buf.at[q, pl.ds(tok, tok), :],
            a_snd.at[q], a_rcv.at[q], partner,
        )

    def tail_local(dx):
        return pltpu.make_async_copy(
            og.at[0, :, tail_of(zh, dx, c)], a2.at[dx, pl.ds(0, tok), :], c_loc.at[dx]
        )

    def tail_load(g, dx):
        z = zh if g == 0 else 1 - zh
        core = c if g == 1 else 1 - c
        return pltpu.make_async_copy(
            og.at[0, :, tail_of(z, dx, core)], tbuf.at[g, dx], t_sem.at[g, dx]
        )

    def tail_remote(g, dx):
        return remote(
            tbuf.at[g, dx], a2.at[dx, pl.ds((g + 1) * tok, tok), :],
            c_snd.at[g, dx], c_rcv.at[g, dx], (partner, opposite, diagonal)[g],
        )

    def window_cols(j, width=SW):
        return pl.ds(pl.multiple_of(j * width, width), width)

    def b_load(j):
        return pltpu.make_async_copy(hid.at[0, :, window_cols(j)], hbuf.at[j], l_sem.at[j])

    def b_load_first(j):
        return pltpu.make_async_copy(emb.at[:, window_cols(j)], hbuf.at[j], l_sem.at[j])

    def b_remote(j):
        return remote(
            hbuf.at[j], b_buf.at[j, pl.ds(0, tok), :],
            b_snd.at[j], b_rcv.at[j], following,
        )

    def e_remote(j):
        return remote(
            hbuf.at[j], b2.at[j, pl.ds(0, tok), :],
            e_snd.at[j], e_rcv.at[j], following2,
        )

    def forward(j):
        return remote(
            b_buf.at[j, pl.ds(0, tok), :], b_buf.at[j, pl.ds(tok, tok), :],
            f_snd.at[j], f_rcv.at[j], partner,
        )

    def forward2(j):
        return remote(
            b2.at[j, pl.ds(0, tok), :], b2.at[j, pl.ds(tok, tok), :],
            h_snd.at[j], h_rcv.at[j], partner,
        )

    def first(d, j, h):
        part = pl.ds(h * SW, SW)
        return remote(
            m1.at[d, j, part, :], r1.at[d, j, part, :],
            m1_snd.at[d, j, h], m1_rcv.at[d, j, h], left if d else right,
        )

    def second(d, z, j):
        return remote(
            m2.at[d, z, j], r2.at[d, z, j], m2_snd.at[d, z, j], m2_rcv.at[d, z, j],
            left if d else right,
        )

    def first2(d, u):
        return remote(
            n1.at[d, u], s1.at[d, u], n1_snd.at[d, u], n1_rcv.at[d, u], left if d else right
        )

    def second2(d, h, u):
        return remote(
            n2.at[d, h, u], s2.at[d, h, u], n2_snd.at[d, h, u], n2_rcv.at[d, h, u],
            left if d else right,
        )

    def last(j):
        return remote(zs.at[j], zr.at[j], z_snd.at[j], z_rcv.at[j], opposite)

    def factor_x(own_z, k):
        z = zh if own_z else 1 - zh
        n = (0 if own_z else nx - 1) + k - 1
        return remote(ag.at[c, z, x], ag.at[c, z, x], g_snd.at[n], g_rcv.at[n], (s, spot(k)))

    def factor_z():
        n = 2 * nx - 2
        return remote(ag.at[c, zh, x], ag.at[c, zh, x], g_snd.at[n], g_rcv.at[n], opposite)

    def factor_c():
        n = 2 * nx - 1
        return remote(ag.at[c], ag.at[c], g_snd.at[n], g_rcv.at[n], partner)

    def store(j):
        return pltpu.make_async_copy(
            obuf.at[j], out.at[0, pl.ds(0, main), window_cols(j, CW)], o_sem.at[j]
        )

    def store2(j):
        return pltpu.make_async_copy(
            obuf2.at[j], out.at[0, pl.ds(main, tail), window_cols(j)], o2_sem.at[j]
        )

    def send_b(j):
        b_load(j).wait()
        b_remote(j).start()

    def take_b(j):
        b_remote(j).wait_recv()
        forward(j).start()
        e_remote(j).start()

    def take_b2(j):
        e_remote(j).wait_recv()
        forward2(j).start()

    def wait_a(*pairs):
        for z, dx in pairs:
            a_local(z, dx).wait()
            a_remote(z, dx).wait_recv()

    load_counts = pltpu.make_async_copy(counts_in, counts, i_sem.at[0])
    load_owners = pltpu.make_async_copy(owners_in, owners, i_sem.at[1])
    def load_b(j, carry):
        @pl.when(s == sections - 1)
        def _():
            b_load_first(j).start()

        @pl.when(s < sections - 1)
        def _():
            b_load(j).start()

        return carry

    lax.fori_loop(0, ns, load_b, 0)
    load_counts.start()
    load_owners.start()
    for z, dx in ((0, 2), (1, 2), (1, 1), (0, 3), (0, 1), (1, 3), (0, 0), (1, 0)):
        a_local(z, dx).start()
    for dx in range(nx):
        tail_local(dx).start()
        for g in range(3):
            tail_load(g, dx).start()
    barrier = pltpu.get_barrier_semaphore()
    neighbours = (
        right, left, across, opposite, partner, diagonal, following, previous, following2, previous2
    )
    for device in neighbours:
        pl.semaphore_signal(barrier, inc=1, device_id=device, device_id_type=MESH)
    ag[c, zh, x] = ainv[0, 0]
    pl.semaphore_wait(barrier, len(neighbours))

    send_b(0)
    factor_z().start()
    for z, dx in ((0, 2), (1, 2), (1, 1), (0, 3), (0, 1), (1, 3)):
        a_remote(z, dx).start()
    for k in range(1, nx):
        factor_x(True, k).start()
    for j in range(1, AHEAD):
        send_b(j)
    load_counts.wait()
    load_owners.wait()
    take_b(0)
    for z, dx in ((0, 0), (1, 0)):
        a_remote(z, dx).start()
    for dx in range(nx):
        tail_load(0, dx).wait()
        tail_remote(0, dx).start()

    def bounds(z, core):
        replica = spot(0, z, core)
        return counts[0, replica], counts[1, replica]

    half = tok // 2

    def transpose(source, target, j, z):
        limits = (*bounds(z, c), *bounds(z, 1 - c))
        for p in range(4):
            piece = source[j, pl.ds(p * half, half), :].astype(F32)
            slots = lax.broadcasted_iota(jnp.int32, piece.shape, 0)
            piece = jnp.where(slots < limits[p], piece, 0.0)
            target[window_cols(j), pl.ds(p * half, half)] = piece.T.astype(BF16)

    def term(j, q):
        return jnp.dot(bt[window_cols(j, CW), :], a_buf[q], preferred_element_type=F32)

    def scale(width):
        total = jnp.int32(0)
        for r in range(counts.shape[0]):
            for m in range(counts.shape[1]):
                total = total + counts[r, m]
        return 1.0 / jnp.sqrt(jnp.full((1, width), total.astype(F32)))

    def choose(t, carry):
        owner = owners[0, t]
        slot = jnp.int32(0)
        for t2 in range(window // size):
            slot = slot + jnp.where((owners[0, t2] == owner) & (t2 < t), 1, 0)
        slot = jnp.minimum(slot, ainv.shape[2] - 1)
        chosen[t] = ag[owner % 2, owner // (2 * nx), (owner // 2) % nx, slot]
        return carry

    def finish(j):
        last(j).wait_recv()
        grad = ((own[j] + zr[j].astype(F32)) * scale(main)).astype(BF16)
        adjusted = jnp.concatenate(
            [
                jnp.dot(grad[:, b * size:(b + 1) * size], ginv[0, b], preferred_element_type=F32)
                for b in range(blocks - 1)
            ],
            axis=1,
        ).astype(BF16)
        for k in range(CW // size):
            piece = jnp.dot(
                chosen[j * (CW // size) + k], adjusted[k * size:(k + 1) * size, :],
                preferred_element_type=F32,
            )
            obuf[j, :, pl.ds(k * size, size)] = piece.T.astype(BF16)
        store(j).start()

    def finish2(u, carry):
        for d in range(2):
            for h in range(2):
                second2(d, h, u).wait_recv()
        weights = scale(tail)
        grad = jnp.concatenate(
            [
                ((own2[u, h] + s2[0, h, u].astype(F32) + s2[1, h, u].astype(F32)) * weights)
                .astype(BF16)
                for h in range(2)
            ],
            axis=0,
        )
        adjusted = jnp.dot(grad, ginv[0, blocks - 1], preferred_element_type=F32).astype(BF16)
        for k in range(uw // size):
            t = u * (uw // size) + k
            piece = jnp.dot(
                chosen[t], adjusted[k * size:(k + 1) * size, :], preferred_element_type=F32
            )
            obuf2[t] = piece.T.astype(BF16)
            store2(t).start()
        return carry

    hw = uw // 2

    def begin2(u, carry):
        cols = pl.ds(pl.multiple_of(u * uw, uw), uw)
        near, far = bt[cols, :], bt2[cols, :]

        def side(start):
            return jnp.concatenate([a2[dx, pl.ds(start, 2 * tok), :] for dx in range(nx)], axis=1)

        value = jnp.dot(near, side(0), preferred_element_type=F32) + jnp.dot(
            far, side(2 * tok), preferred_element_type=F32
        )

        def block(h, dx):
            return value[h * hw:(h + 1) * hw, dx * tail:(dx + 1) * tail]

        for d in range(2):
            n1[d, u] = block(d, 2).astype(BF16)
            first2(d, u).start()
        for d, dx in ((0, 1), (1, nx - 1)):
            comb[d, u] = block(d, dx)
            n2[d, 1 - d, u] = block(1 - d, dx).astype(BF16)
        for h in range(2):
            own2[u, h] = block(h, 0)
        return carry

    def middle2(u, carry):
        for d in range(2):
            second2(d, 1 - d, u).start()
        for d in range(2):
            first2(d, u).wait_recv()
            n2[d, d, u] = (comb[d, u] + s1[d, u].astype(F32)).astype(BF16)
            second2(d, d, u).start()
        return carry

    def step(i, carry):
        @pl.when(i >= 2)
        def _():
            j = i - 2

            @pl.when(i == 2)
            def _():
                wait_a((0, 1), (1, 3))

            for d, q in ((0, 1), (1, nx + 3)):
                value = term(j, q)
                for h in range(SUBS):
                    first(d, j, h).wait_recv()
                m2[d, d, j] = (value + r1[d, j].astype(F32)).astype(BF16)
                second(d, d, j).start()

        @pl.when(i == 0)
        def _():
            wait_a((0, 2), (1, 2))
            for h in range(SUBS):
                if h:
                    take_b(h)
                forward(h).wait_recv()
                transpose(b_buf, bt, h, zh)
                for d, q in ((0, 2), (1, nx + 2)):
                    part = bt[pl.ds(h * SW, SW), :]
                    m1[d, 0, pl.ds(h * SW, SW), :] = jnp.dot(
                        part, a_buf[q], preferred_element_type=F32
                    ).astype(BF16)
                    first(d, 0, h).start()

        @pl.when((i > 0) & (i < nc))
        def _():
            for h in range(SUBS):
                forward(i * SUBS + h).wait_recv()
                transpose(b_buf, bt, i * SUBS + h, zh)
            for d, q in ((0, 2), (1, nx + 2)):
                m1[d, i] = term(i, q).astype(BF16)
                for h in range(SUBS):
                    first(d, i, h).start()

        @pl.when((i >= 1) & (i < nc + 1))
        def _():
            @pl.when(i == 1)
            def _():
                wait_a((1, 1), (0, 3))

            j = i - 1
            for d, q in ((0, nx + 1), (1, 3)):
                m2[d, 1 - d, j] = term(j, q).astype(BF16)
                second(d, 1 - d, j).start()

        @pl.when(i * SUBS + AHEAD < ns)
        def _():
            for h in range(SUBS):
                send_b(i * SUBS + AHEAD + h)

        pieces = [(g, dx) for g in (1, 2) for dx in range(nx)]
        for n, count in enumerate(PACE):
            @pl.when(i == n)
            def _():
                for g, dx in pieces[sum(PACE[:n]):sum(PACE[:n]) + count]:
                    tail_load(g, dx).wait()
                    tail_remote(g, dx).start()

        @pl.when(i + 1 < nc)
        def _():
            for h in range(SUBS):
                take_b((i + 1) * SUBS + h)

        @pl.when(i == 2)
        def _():
            factor_z().wait_recv()
            for k in range(1, nx):
                factor_x(False, k).start()

        @pl.when(i == 3)
        def _():
            for k in range(1, nx):
                factor_x(True, k).wait_recv()
                factor_x(False, k).wait_recv()
            factor_c().start()

        @pl.when((i >= 1) & (i < nc + 1))
        def _():
            for h in range(SUBS):
                forward2((i - 1) * SUBS + h).wait_recv()
                transpose(b2, bt2, (i - 1) * SUBS + h, 1 - zh)

        @pl.when(i == nc)
        def _():
            for dx in range(nx):
                tail_local(dx).wait()
                for g in range(3):
                    tail_remote(g, dx).wait_recv()
            lax.fori_loop(0, nu, begin2, 0)

        @pl.when(i == nc + 1)
        def _():
            lax.fori_loop(0, nu, middle2, 0)

        @pl.when(i >= 2)
        def _():
            j = i - 2

            @pl.when(i == 2)
            def _():
                wait_a((0, 0), (1, 0))

            away = term(j, (1 - zh) * nx)
            mine = term(j, zh * nx)
            second(0, 1, j).wait_recv()
            second(1, 0, j).wait_recv()
            second(0, 0, j).wait_recv()
            second(1, 1, j).wait_recv()
            zs[j] = (
                away + r2[0, 1 - zh, j].astype(F32) + r2[1, 1 - zh, j].astype(F32)
            ).astype(BF16)
            last(j).start()
            own[j] = mine + r2[0, zh, j].astype(F32) + r2[1, zh, j].astype(F32)

        @pl.when(i < nc)
        def _():
            for h in range(SUBS):
                take_b2(i * SUBS + h)

        @pl.when(i == 2 + LAG)
        def _():
            factor_c().wait_recv()
            lax.fori_loop(0, window // size, choose, 0)

        @pl.when(i >= 2 + LAG)
        def _():
            finish(i - 2 - LAG)

        return carry

    lax.fori_loop(0, nc + 2, step, 0)

    def rest(j, carry):
        finish(j)
        return carry

    lax.fori_loop(nc - LAG, nc, rest, 0)
    lax.fori_loop(0, nu, finish2, 0)

    for dx in range(nx):
        for z in range(2):
            a_remote(z, dx).wait_send()
        for g in range(3):
            tail_remote(g, dx).wait_send()
    for k in range(1, nx):
        factor_x(True, k).wait_send()
        factor_x(False, k).wait_send()
    factor_z().wait_send()
    factor_c().wait_send()

    def drain(j, carry):
        b_remote(j).wait_send()
        e_remote(j).wait_send()

        forward(j).wait_send()
        forward2(j).wait_send()
        store2(j).wait()
        return carry

    lax.fori_loop(0, ns, drain, 0)

    def drain1(j, carry):
        for d in range(2):
            for h in range(SUBS):
                first(d, j, h).wait_send()
            for z in range(2):
                second(d, z, j).wait_send()
        last(j).wait_send()
        store(j).wait()
        return carry

    lax.fori_loop(0, nc, drain1, 0)

    def drain2(u, carry):
        for d in range(2):
            first2(d, u).wait_send()
            for h in range(2):
                second2(d, h, u).wait_send()
        return carry

    lax.fori_loop(0, nu, drain2, 0)


def local(sections, groups, embedded, hidden_out, out_grads, counts, owners, ginv, ainv):
    tok, window = embedded.shape
    rows = out_grads.shape[-1] // groups
    size = ginv.shape[-1]
    main = rows - size
    nx = groups // 4
    nc, ns, nu = window // CW, window // SW, window // UW
    hw = UW // 2
    dims = (sections, nx, rows, tok, window)
    hbm = pl.BlockSpec(memory_space=pl.ANY)
    vmem = pl.BlockSpec(memory_space=pltpu.VMEM)
    dma = pltpu.SemaphoreType.DMA
    flops = 2 * tok * out_grads.shape[-1] * window
    return pl.pallas_call(
        functools.partial(kernel, dims),
        out_shape=jax.ShapeDtypeStruct((1, rows, window), BF16),
        in_specs=[hbm, hbm, hbm, hbm, hbm, vmem, vmem],
        out_specs=hbm,
        scratch_shapes=[
            pltpu.SMEM(counts.shape[::-1], jnp.int32),
            pltpu.SMEM(owners.shape[:2], jnp.int32),
            pltpu.VMEM((2 * nx, 2 * tok, main), BF16),
            pltpu.VMEM((nx, 4 * tok, size), BF16),
            pltpu.VMEM((ns, 2 * tok, SW), BF16),
            pltpu.VMEM((ns, 2 * tok, SW), BF16),
            pltpu.VMEM((window, 2 * tok), BF16),
            pltpu.VMEM((window, 2 * tok), BF16),
            pltpu.VMEM((2, nc, CW, main), BF16),
            pltpu.VMEM((2, nc, CW, main), BF16),
            pltpu.VMEM((2, 2, nc, CW, main), BF16),
            pltpu.VMEM((2, 2, nc, CW, main), BF16),
            pltpu.VMEM((nc, CW, main), F32),
            pltpu.VMEM((nc, CW, main), BF16),
            pltpu.VMEM((nc, CW, main), BF16),
            pltpu.VMEM((2, nu, hw, size), BF16),
            pltpu.VMEM((2, nu, hw, size), BF16),
            pltpu.VMEM((2, 2, nu, hw, size), BF16),
            pltpu.VMEM((2, 2, nu, hw, size), BF16),
            pltpu.VMEM((2, nu, hw, size), F32),
            pltpu.VMEM((nu, 2, hw, size), F32),
            pltpu.VMEM((2, 2, nx) + ainv.shape[2:], BF16),
            pltpu.VMEM((window // size, size, size), BF16),
            pltpu.VMEM((nc, main, CW), BF16),
            pltpu.VMEM((ns, size, SW), BF16),
            pltpu.VMEM((ns, tok, SW), BF16),
            pltpu.VMEM((3, nx, tok, size), BF16),
            dma((2,)), dma((ns,)), dma((3, nx)), dma((2 * nx,)), dma((2 * nx,)), dma((2 * nx,)),
            dma((nx,)), dma((3, nx)), dma((3, nx)),
            dma((ns,)), dma((ns,)), dma((ns,)), dma((ns,)), dma((ns,)), dma((ns,)),
            dma((ns,)), dma((ns,)),
            dma((2, nc, SUBS)), dma((2, nc, SUBS)), dma((2, 2, nc)), dma((2, 2, nc)),
            dma((2, nu)), dma((2, nu)), dma((2, 2, nu)), dma((2, 2, nu)),
            dma((nc,)), dma((nc,)), dma((2 * nx,)), dma((2 * nx,)), dma((nc,)), dma((ns,)),
        ],
        compiler_params=pltpu.CompilerParams(
            collective_id=0, has_side_effects=True, vmem_limit_bytes=60 << 20
        ),
        cost_estimate=pl.CostEstimate(
            flops=flops, bytes_accessed=2 * out_grads.size, transcendentals=0
        ),
    )(embedded, hidden_out, out_grads, counts.T, owners[:, :, 0], ginv, ainv)


def solution(mesh):
    placed = (
        P("dp", None),
        P("section", "dp", None),
        P("section", "dp", None),
        P(),
        P("section", None, None),
        P("section", "dp", None, None),
        P("section", "dp", None, None, None),
    )
    return jax.shard_map(
        functools.partial(local, mesh.shape["section"], mesh.shape["dp"]),
        mesh=mesh, in_specs=placed, out_specs=P("section", "dp", None), check_vma=False,
    )
```

```python
import functools

import jax
import jax.numpy as jnp
from jax import lax
from jax.experimental import pallas as pl
from jax.experimental.pallas import tpu as pltpu
from jax.sharding import PartitionSpec as P

MESH = pl.DeviceIdType.MESH
F32 = jnp.float32
BF16 = jnp.bfloat16

SW = 128
SUBS = 2
CW = SUBS * SW
UW = 512
AHEAD = 4
EARLY = 4
PIECES2 = ((0, 2), (2, 6), (6, 10), (10, 12))
LAG = 3
PACE = (2, 2, 1, 1, 1, 1)


def kernel(
    dims, emb, hid, og, counts_in, owners_in, ginv, ainv, out,
    counts, owners, a_buf, a2, b_buf, b2, bt, bt2, m1, r1, m2, r2, own, zs, zr,
    n1, s1, n2, s2, comb, own2, ag, chosen, obuf, obuf2, hbuf, tbuf, relay,
    i_sem, l_sem, t_sem, k_snd, k_rcv, a_loc, a_snd, a_rcv, c_loc, c_snd, c_rcv, b_snd, b_rcv, e_snd, e_rcv, f_snd, f_rcv,
    h_snd, h_rcv, m1_snd, m1_rcv, m2_snd, m2_rcv, n1_snd, n1_rcv, n2_snd, n2_rcv,
    z_snd, z_rcv, g_snd, g_rcv, o_sem, o2_sem,
):
    sections, nx, rows, tok, window = dims
    nc = window // CW
    ns = window // SW
    nu = window // UW
    uw = UW
    size = ginv.shape[-1]
    blocks = ginv.shape[1]
    tail = size
    main = rows - tail
    s = lax.axis_index("section")
    dp = lax.axis_index("dp")
    zh, x, c = dp // (2 * nx), (dp // 2) % nx, dp % 2

    def spot(dx=0, z=None, core=None):
        z = zh if z is None else z
        core = c if core is None else core
        return (z * nx + (x + dx) % nx) * 2 + core

    right, left, across = (s, spot(1)), (s, spot(nx - 1)), (s, spot(2))
    opposite, partner = (s, spot(z=1 - zh)), (s, spot(core=1 - c))
    diagonal = (s, spot(z=1 - zh, core=1 - c))
    following, previous = ((s + 1) % sections, dp), ((s + sections - 1) % sections, dp)
    even = s % 2 == 0
    beside = (s // 2 * 2 + 1 - s % 2, opposite[1])
    skipped, skipping = ((s + 2) % sections, dp), ((s + sections - 2) % sections, dp)

    def remote(src, dst, snd, rcv, device):
        return pltpu.make_async_remote_copy(
            src_ref=src, dst_ref=dst, send_sem=snd, recv_sem=rcv,
            device_id=device, device_id_type=MESH,
        )

    def main_of(z, dx, core):
        return pl.ds(pl.multiple_of(spot(dx, z, core) * rows, rows), main)

    def tail_of(z, dx, core):
        return pl.ds(pl.multiple_of(spot(dx, z, core) * rows + main, tail), tail)

    def a_local(z, dx):
        q = z * nx + dx
        return pltpu.make_async_copy(
            og.at[0, :, main_of(z, dx, c)], a_buf.at[q, pl.ds(0, tok), :], a_loc.at[q]
        )

    def a_remote(z, dx):
        q = z * nx + dx
        return remote(
            og.at[0, :, main_of(z, dx, 1 - c)], a_buf.at[q, pl.ds(tok, tok), :],
            a_snd.at[q], a_rcv.at[q], partner,
        )

    def tail_local(dx):
        return pltpu.make_async_copy(
            og.at[0, :, tail_of(zh, dx, c)], a2.at[dx, pl.ds(0, tok), :], c_loc.at[dx]
        )

    def tail_load(g, dx):
        z = zh if g == 0 else 1 - zh
        core = c if g == 1 else 1 - c
        return pltpu.make_async_copy(
            og.at[0, :, tail_of(z, dx, core)], tbuf.at[g, dx], t_sem.at[g, dx]
        )

    def tail_remote(g, dx):
        return remote(
            tbuf.at[g, dx], a2.at[dx, pl.ds((g + 1) * tok, tok), :],
            c_snd.at[g, dx], c_rcv.at[g, dx], (partner, opposite, diagonal)[g],
        )

    def window_cols(j, width=SW):
        return pl.ds(pl.multiple_of(j * width, width), width)

    def b_load(j):
        return pltpu.make_async_copy(hid.at[0, :, window_cols(j)], hbuf.at[j], l_sem.at[j])

    def b_load_first(j):
        return pltpu.make_async_copy(emb.at[:, window_cols(j)], hbuf.at[j], l_sem.at[j])

    def b_remote(j):
        return remote(
            hbuf.at[j], b_buf.at[j, pl.ds(0, tok), :],
            b_snd.at[j], b_rcv.at[j], following,
        )

    def e_direct(j):
        return remote(
            hbuf.at[j], b2.at[j, pl.ds(0, tok), :], e_snd.at[j], e_rcv.at[j], beside
        )

    def e_relay(j):
        return remote(hbuf.at[j], relay.at[j], e_snd.at[j], k_rcv.at[j], beside)

    def e_pass(j):
        return remote(
            relay.at[j], b2.at[j, pl.ds(0, tok), :], k_snd.at[j], e_rcv.at[j], skipped
        )

    def forward(j):
        return remote(
            b_buf.at[j, pl.ds(0, tok), :], b_buf.at[j, pl.ds(tok, tok), :],
            f_snd.at[j], f_rcv.at[j], partner,
        )

    def forward2(j):
        return remote(
            b2.at[j, pl.ds(0, tok), :], b2.at[j, pl.ds(tok, tok), :],
            h_snd.at[j], h_rcv.at[j], partner,
        )

    def first(d, j, h):
        part = pl.ds(h * SW, SW)
        return remote(
            m1.at[d, j, part, :], r1.at[d, j, part, :],
            m1_snd.at[d, j, h], m1_rcv.at[d, j, h], left if d else right,
        )

    def second(d, z, j):
        return remote(
            m2.at[d, z, j], r2.at[d, z, j], m2_snd.at[d, z, j], m2_rcv.at[d, z, j],
            left if d else right,
        )

    def first2(d, u):
        return remote(
            n1.at[d, u], s1.at[d, u], n1_snd.at[d, u], n1_rcv.at[d, u], left if d else right
        )

    def second2(d, h, u):
        return remote(
            n2.at[d, h, u], s2.at[d, h, u], n2_snd.at[d, h, u], n2_rcv.at[d, h, u],
            left if d else right,
        )

    def last(j):
        return remote(zs.at[j], zr.at[j], z_snd.at[j], z_rcv.at[j], opposite)

    def factor_x(own_z, k):
        z = zh if own_z else 1 - zh
        n = (0 if own_z else nx - 1) + k - 1
        return remote(ag.at[c, z, x], ag.at[c, z, x], g_snd.at[n], g_rcv.at[n], (s, spot(k)))

    def factor_z():
        n = 2 * nx - 2
        return remote(ag.at[c, zh, x], ag.at[c, zh, x], g_snd.at[n], g_rcv.at[n], opposite)

    def factor_c():
        n = 2 * nx - 1
        return remote(ag.at[c], ag.at[c], g_snd.at[n], g_rcv.at[n], partner)

    def store(j):
        return pltpu.make_async_copy(
            obuf.at[j], out.at[0, pl.ds(0, main), window_cols(j, CW)], o_sem.at[j]
        )

    def store2(j):
        return pltpu.make_async_copy(
            obuf2.at[j], out.at[0, pl.ds(main, tail), window_cols(j)], o2_sem.at[j]
        )

    def send_b(j):
        b_remote(j).start()

    def take_b(j):
        b_remote(j).wait_recv()
        forward(j).start()

    def send_b2(j):
        @pl.when(even)
        def _():
            e_direct(j).start()

        @pl.when(jnp.logical_not(even))
        def _():
            e_relay(j).start()

    def pass_b2(j):
        @pl.when(even)
        def _():
            e_relay(j).wait_recv()
            e_pass(j).start()

    def take_b2(j):
        @pl.when(even)
        def _():
            e_pass(j).wait_recv()

        @pl.when(jnp.logical_not(even))
        def _():
            e_direct(j).wait_recv()

        forward2(j).start()

    def wait_a(*pairs):
        for z, dx in pairs:
            a_local(z, dx).wait()
            a_remote(z, dx).wait_recv()

    load_counts = pltpu.make_async_copy(counts_in, counts, i_sem.at[0])
    load_owners = pltpu.make_async_copy(owners_in, owners, i_sem.at[1])
    def load_b(j, carry):
        @pl.when(s == sections - 1)
        def _():
            b_load_first(j).start()

        @pl.when(s < sections - 1)
        def _():
            b_load(j).start()

        return carry

    lax.fori_loop(0, ns, load_b, 0)
    load_counts.start()
    load_owners.start()
    for z, dx in ((0, 2), (1, 2), (1, 1), (0, 3), (0, 1), (1, 3), (0, 0), (1, 0)):
        a_local(z, dx).start()
    for dx in range(nx):
        tail_local(dx).start()
        for g in range(3):
            tail_load(g, dx).start()
    barrier = pltpu.get_barrier_semaphore()
    neighbours = (
        right, left, across, opposite, partner, diagonal, following, previous,
        beside, skipped, skipping,
    )
    for device in neighbours:
        pl.semaphore_signal(barrier, inc=1, device_id=device, device_id_type=MESH)
    ag[c, zh, x] = ainv[0, 0]
    pl.semaphore_wait(barrier, len(neighbours))

    b_load(0).wait()
    send_b(0)
    factor_z().start()
    for z, dx in ((0, 2), (1, 2), (1, 1), (0, 3), (0, 1), (1, 3)):
        a_remote(z, dx).start()
    for k in range(1, nx):
        factor_x(True, k).start()
    send_b2(0)
    for j in range(1, EARLY):
        b_load(j).wait()
        send_b(j)
        send_b2(j)
    load_counts.wait()
    load_owners.wait()
    take_b(0)
    for z, dx in ((0, 0), (1, 0)):
        a_remote(z, dx).start()
    for j in range(EARLY, ns):
        b_load(j).wait()
        if j < AHEAD:
            send_b(j)
        send_b2(j)
    for dx in range(nx):
        tail_load(0, dx).wait()
        tail_remote(0, dx).start()

    def bounds(z, core):
        replica = spot(0, z, core)
        return counts[0, replica], counts[1, replica]

    half = tok // 2

    def transpose(source, target, j, z):
        limits = (*bounds(z, c), *bounds(z, 1 - c))
        for p in range(4):
            piece = source[j, pl.ds(p * half, half), :].astype(F32)
            slots = lax.broadcasted_iota(jnp.int32, piece.shape, 0)
            piece = jnp.where(slots < limits[p], piece, 0.0)
            target[window_cols(j), pl.ds(p * half, half)] = piece.T.astype(BF16)

    def term(j, q):
        return jnp.dot(bt[window_cols(j, CW), :], a_buf[q], preferred_element_type=F32)

    def scale(width):
        total = jnp.int32(0)
        for r in range(counts.shape[0]):
            for m in range(counts.shape[1]):
                total = total + counts[r, m]
        return 1.0 / jnp.sqrt(jnp.full((1, width), total.astype(F32)))

    def choose(t, carry):
        owner = owners[0, t]
        slot = jnp.int32(0)
        for t2 in range(window // size):
            slot = slot + jnp.where((owners[0, t2] == owner) & (t2 < t), 1, 0)
        slot = jnp.minimum(slot, ainv.shape[2] - 1)
        chosen[t] = ag[owner % 2, owner // (2 * nx), (owner // 2) % nx, slot]
        return carry

    def finish(j):
        last(j).wait_recv()
        grad = ((own[j] + zr[j].astype(F32)) * scale(main)).astype(BF16)
        adjusted = jnp.concatenate(
            [
                jnp.dot(grad[:, b * size:(b + 1) * size], ginv[0, b], preferred_element_type=F32)
                for b in range(blocks - 1)
            ],
            axis=1,
        ).astype(BF16)
        for k in range(CW // size):
            piece = jnp.dot(
                chosen[j * (CW // size) + k], adjusted[k * size:(k + 1) * size, :],
                preferred_element_type=F32,
            )
            obuf[j, :, pl.ds(k * size, size)] = piece.T.astype(BF16)
        store(j).start()

    def finish2(u, carry):
        for d in range(2):
            for h in range(2):
                second2(d, h, u).wait_recv()
        weights = scale(tail)
        grad = jnp.concatenate(
            [
                ((own2[u, h] + s2[0, h, u].astype(F32) + s2[1, h, u].astype(F32)) * weights)
                .astype(BF16)
                for h in range(2)
            ],
            axis=0,
        )
        adjusted = jnp.dot(grad, ginv[0, blocks - 1], preferred_element_type=F32).astype(BF16)
        for k in range(uw // size):
            t = u * (uw // size) + k
            piece = jnp.dot(
                chosen[t], adjusted[k * size:(k + 1) * size, :], preferred_element_type=F32
            )
            obuf2[t] = piece.T.astype(BF16)
            store2(t).start()
        return carry

    hw = uw // 2

    def begin2(u, carry):
        cols = pl.ds(pl.multiple_of(u * uw, uw), uw)
        near, far = bt[cols, :], bt2[cols, :]

        def side(start):
            return jnp.concatenate([a2[dx, pl.ds(start, 2 * tok), :] for dx in range(nx)], axis=1)

        value = jnp.dot(near, side(0), preferred_element_type=F32) + jnp.dot(
            far, side(2 * tok), preferred_element_type=F32
        )

        def block(h, dx):
            return value[h * hw:(h + 1) * hw, dx * tail:(dx + 1) * tail]

        for d in range(2):
            n1[d, u] = block(d, 2).astype(BF16)
            first2(d, u).start()
        for d, dx in ((0, 1), (1, nx - 1)):
            comb[d, u] = block(d, dx)
            n2[d, 1 - d, u] = block(1 - d, dx).astype(BF16)
        for h in range(2):
            own2[u, h] = block(h, 0)
        return carry

    def middle2(u, carry):
        for d in range(2):
            second2(d, 1 - d, u).start()
        for d in range(2):
            first2(d, u).wait_recv()
            n2[d, d, u] = (comb[d, u] + s1[d, u].astype(F32)).astype(BF16)
            second2(d, d, u).start()
        return carry

    def step(i, carry):
        @pl.when(i >= 2)
        def _():
            j = i - 2

            @pl.when(i == 2)
            def _():
                wait_a((0, 1), (1, 3))

            for d, q in ((0, 1), (1, nx + 3)):
                value = term(j, q)
                for h in range(SUBS):
                    first(d, j, h).wait_recv()
                m2[d, d, j] = (value + r1[d, j].astype(F32)).astype(BF16)
                second(d, d, j).start()

        @pl.when(i == 0)
        def _():
            wait_a((0, 2), (1, 2))
            for h in range(SUBS):
                if h:
                    take_b(h)
                forward(h).wait_recv()
                transpose(b_buf, bt, h, zh)
                for d, q in ((0, 2), (1, nx + 2)):
                    part = bt[pl.ds(h * SW, SW), :]
                    m1[d, 0, pl.ds(h * SW, SW), :] = jnp.dot(
                        part, a_buf[q], preferred_element_type=F32
                    ).astype(BF16)
                    first(d, 0, h).start()

        @pl.when((i > 0) & (i < nc))
        def _():
            for h in range(SUBS):
                forward(i * SUBS + h).wait_recv()
                transpose(b_buf, bt, i * SUBS + h, zh)
            for d, q in ((0, 2), (1, nx + 2)):
                m1[d, i] = term(i, q).astype(BF16)
                for h in range(SUBS):
                    first(d, i, h).start()

        @pl.when((i >= 1) & (i < nc + 1))
        def _():
            @pl.when(i == 1)
            def _():
                wait_a((1, 1), (0, 3))

            j = i - 1
            for d, q in ((0, nx + 1), (1, 3)):
                m2[d, 1 - d, j] = term(j, q).astype(BF16)
                second(d, 1 - d, j).start()

        @pl.when(i * SUBS + AHEAD < ns)
        def _():
            for h in range(SUBS):
                send_b(i * SUBS + AHEAD + h)

        pieces = [(g, dx) for g in (1, 2) for dx in range(nx)]
        for n, count in enumerate(PACE):
            @pl.when(i == n)
            def _():
                for g, dx in pieces[sum(PACE[:n]):sum(PACE[:n]) + count]:
                    tail_load(g, dx).wait()
                    tail_remote(g, dx).start()

        @pl.when(i + 1 < nc)
        def _():
            for h in range(SUBS):
                take_b((i + 1) * SUBS + h)

        @pl.when(i == 3)
        def _():
            factor_z().wait_recv()
            for k in range(1, nx):
                factor_x(False, k).start()

        @pl.when(i == 4)
        def _():
            for k in range(1, nx):
                factor_x(True, k).wait_recv()
                factor_x(False, k).wait_recv()
            factor_c().start()

        for n, (low, high) in enumerate(PIECES2):
            @pl.when(i == n + 3)
            def _():
                for j in range(low, high):
                    forward2(j).wait_recv()
                    transpose(b2, bt2, j, 1 - zh)

        @pl.when(i == nc)
        def _():
            for dx in range(nx):
                tail_local(dx).wait()
                for g in range(3):
                    tail_remote(g, dx).wait_recv()
            lax.fori_loop(0, nu, begin2, 0)

        @pl.when(i == nc + 1)
        def _():
            lax.fori_loop(0, nu, middle2, 0)

        @pl.when(i >= 2)
        def _():
            j = i - 2

            @pl.when(i == 2)
            def _():
                wait_a((0, 0), (1, 0))

            away = term(j, (1 - zh) * nx)
            mine = term(j, zh * nx)
            second(0, 1, j).wait_recv()
            second(1, 0, j).wait_recv()
            second(0, 0, j).wait_recv()
            second(1, 1, j).wait_recv()
            zs[j] = (
                away + r2[0, 1 - zh, j].astype(F32) + r2[1, 1 - zh, j].astype(F32)
            ).astype(BF16)
            last(j).start()
            own[j] = mine + r2[0, zh, j].astype(F32) + r2[1, zh, j].astype(F32)

        for n, (low, high) in enumerate(PIECES2):
            @pl.when(i == n + 1)
            def _():
                for j in range(low, high):
                    pass_b2(j)

            @pl.when(i == n + 2)
            def _():
                for j in range(low, high):
                    take_b2(j)

        @pl.when(i == 2 + LAG)
        def _():
            factor_c().wait_recv()
            lax.fori_loop(0, window // size, choose, 0)

        @pl.when(i >= 2 + LAG)
        def _():
            finish(i - 2 - LAG)

        return carry

    lax.fori_loop(0, nc + 2, step, 0)

    def rest(j, carry):
        finish(j)
        return carry

    lax.fori_loop(nc - LAG, nc, rest, 0)
    lax.fori_loop(0, nu, finish2, 0)

    for dx in range(nx):
        for z in range(2):
            a_remote(z, dx).wait_send()
        for g in range(3):
            tail_remote(g, dx).wait_send()
    for k in range(1, nx):
        factor_x(True, k).wait_send()
        factor_x(False, k).wait_send()
    factor_z().wait_send()
    factor_c().wait_send()

    def drain(j, carry):
        b_remote(j).wait_send()

        @pl.when(even)
        def _():
            e_direct(j).wait_send()
            e_pass(j).wait_send()

        @pl.when(jnp.logical_not(even))
        def _():
            e_relay(j).wait_send()


        forward(j).wait_send()
        forward2(j).wait_send()
        store2(j).wait()
        return carry

    lax.fori_loop(0, ns, drain, 0)

    def drain1(j, carry):
        for d in range(2):
            for h in range(SUBS):
                first(d, j, h).wait_send()
            for z in range(2):
                second(d, z, j).wait_send()
        last(j).wait_send()
        store(j).wait()
        return carry

    lax.fori_loop(0, nc, drain1, 0)

    def drain2(u, carry):
        for d in range(2):
            first2(d, u).wait_send()
            for h in range(2):
                second2(d, h, u).wait_send()
        return carry

    lax.fori_loop(0, nu, drain2, 0)


def local(sections, groups, embedded, hidden_out, out_grads, counts, owners, ginv, ainv):
    tok, window = embedded.shape
    rows = out_grads.shape[-1] // groups
    size = ginv.shape[-1]
    main = rows - size
    nx = groups // 4
    nc, ns, nu = window // CW, window // SW, window // UW
    hw = UW // 2
    dims = (sections, nx, rows, tok, window)
    hbm = pl.BlockSpec(memory_space=pl.ANY)
    vmem = pl.BlockSpec(memory_space=pltpu.VMEM)
    dma = pltpu.SemaphoreType.DMA
    flops = 2 * tok * out_grads.shape[-1] * window
    return pl.pallas_call(
        functools.partial(kernel, dims),
        out_shape=jax.ShapeDtypeStruct((1, rows, window), BF16),
        in_specs=[hbm, hbm, hbm, hbm, hbm, vmem, vmem],
        out_specs=hbm,
        scratch_shapes=[
            pltpu.SMEM(counts.shape[::-1], jnp.int32),
            pltpu.SMEM(owners.shape[:2], jnp.int32),
            pltpu.VMEM((2 * nx, 2 * tok, main), BF16),
            pltpu.VMEM((nx, 4 * tok, size), BF16),
            pltpu.VMEM((ns, 2 * tok, SW), BF16),
            pltpu.VMEM((ns, 2 * tok, SW), BF16),
            pltpu.VMEM((window, 2 * tok), BF16),
            pltpu.VMEM((window, 2 * tok), BF16),
            pltpu.VMEM((2, nc, CW, main), BF16),
            pltpu.VMEM((2, nc, CW, main), BF16),
            pltpu.VMEM((2, 2, nc, CW, main), BF16),
            pltpu.VMEM((2, 2, nc, CW, main), BF16),
            pltpu.VMEM((nc, CW, main), F32),
            pltpu.VMEM((nc, CW, main), BF16),
            pltpu.VMEM((nc, CW, main), BF16),
            pltpu.VMEM((2, nu, hw, size), BF16),
            pltpu.VMEM((2, nu, hw, size), BF16),
            pltpu.VMEM((2, 2, nu, hw, size), BF16),
            pltpu.VMEM((2, 2, nu, hw, size), BF16),
            pltpu.VMEM((2, nu, hw, size), F32),
            pltpu.VMEM((nu, 2, hw, size), F32),
            pltpu.VMEM((2, 2, nx) + ainv.shape[2:], BF16),
            pltpu.VMEM((window // size, size, size), BF16),
            pltpu.VMEM((nc, main, CW), BF16),
            pltpu.VMEM((ns, size, SW), BF16),
            pltpu.VMEM((ns, tok, SW), BF16),
            pltpu.VMEM((3, nx, tok, size), BF16),
            pltpu.VMEM((ns, tok, SW), BF16),
            dma((2,)), dma((ns,)), dma((3, nx)), dma((ns,)), dma((ns,)), dma((2 * nx,)), dma((2 * nx,)), dma((2 * nx,)),
            dma((nx,)), dma((3, nx)), dma((3, nx)),
            dma((ns,)), dma((ns,)), dma((ns,)), dma((ns,)), dma((ns,)), dma((ns,)),
            dma((ns,)), dma((ns,)),
            dma((2, nc, SUBS)), dma((2, nc, SUBS)), dma((2, 2, nc)), dma((2, 2, nc)),
            dma((2, nu)), dma((2, nu)), dma((2, 2, nu)), dma((2, 2, nu)),
            dma((nc,)), dma((nc,)), dma((2 * nx,)), dma((2 * nx,)), dma((nc,)), dma((ns,)),
        ],
        compiler_params=pltpu.CompilerParams(
            collective_id=0, has_side_effects=True, vmem_limit_bytes=60 << 20
        ),
        cost_estimate=pl.CostEstimate(
            flops=flops, bytes_accessed=2 * out_grads.size, transcendentals=0
        ),
    )(embedded, hidden_out, out_grads, counts.T, owners[:, :, 0], ginv, ainv)


def solution(mesh):
    placed = (
        P("dp", None),
        P("section", "dp", None),
        P("section", "dp", None),
        P(),
        P("section", None, None),
        P("section", "dp", None, None),
        P("section", "dp", None, None, None),
    )
    return jax.shard_map(
        functools.partial(local, mesh.shape["section"], mesh.shape["dp"]),
        mesh=mesh, in_specs=placed, out_specs=P("section", "dp", None), check_vma=False,
    )
```

```python
import functools

import jax
import jax.numpy as jnp
from jax import lax
from jax.experimental import pallas as pl
from jax.experimental.pallas import tpu as pltpu
from jax.sharding import PartitionSpec as P

MESH = pl.DeviceIdType.MESH
F32 = jnp.float32
BF16 = jnp.bfloat16

SW = 128
SUBS = 2
CW = SUBS * SW
UW = 512
AHEAD = 4
EARLY = 4
PIECES2 = ((0, 2), (2, 6), (6, 10), (10, 12))
LAG = 2
PACE = (2, 2, 1, 1, 1, 1)


def kernel(
    dims, emb, hid, og, counts_in, owners_in, ginv, ainv, out,
    counts, owners, a_buf, a2, b_buf, b2, bt, bt2, m1, r1, m2, r2, own, zs, zr,
    n1, s1, n2, s2, comb, own2, ag, chosen, obuf, obuf2, hbuf, tbuf, relay,
    i_sem, l_sem, t_sem, k_snd, k_rcv, a_loc, a_snd, a_rcv, c_loc, c_snd, c_rcv, b_snd, b_rcv, e_snd, e_rcv, f_snd, f_rcv,
    h_snd, h_rcv, m1_snd, m1_rcv, m2_snd, m2_rcv, n1_snd, n1_rcv, n2_snd, n2_rcv,
    z_snd, z_rcv, g_snd, g_rcv, o_sem, o2_sem,
):
    sections, nx, rows, tok, window = dims
    nc = window // CW
    ns = window // SW
    nu = window // UW
    uw = UW
    size = ginv.shape[-1]
    blocks = ginv.shape[1]
    tail = size
    main = rows - tail
    s = lax.axis_index("section")
    dp = lax.axis_index("dp")
    zh, x, c = dp // (2 * nx), (dp // 2) % nx, dp % 2

    def spot(dx=0, z=None, core=None):
        z = zh if z is None else z
        core = c if core is None else core
        return (z * nx + (x + dx) % nx) * 2 + core

    right, left, across = (s, spot(1)), (s, spot(nx - 1)), (s, spot(2))
    opposite, partner = (s, spot(z=1 - zh)), (s, spot(core=1 - c))
    diagonal = (s, spot(z=1 - zh, core=1 - c))
    following, previous = ((s + 1) % sections, dp), ((s + sections - 1) % sections, dp)
    even = s % 2 == 0
    beside = (s // 2 * 2 + 1 - s % 2, opposite[1])
    skipped, skipping = ((s + 2) % sections, dp), ((s + sections - 2) % sections, dp)

    def remote(src, dst, snd, rcv, device):
        return pltpu.make_async_remote_copy(
            src_ref=src, dst_ref=dst, send_sem=snd, recv_sem=rcv,
            device_id=device, device_id_type=MESH,
        )

    def main_of(z, dx, core):
        return pl.ds(pl.multiple_of(spot(dx, z, core) * rows, rows), main)

    def tail_of(z, dx, core):
        return pl.ds(pl.multiple_of(spot(dx, z, core) * rows + main, tail), tail)

    def a_local(z, dx):
        q = z * nx + dx
        return pltpu.make_async_copy(
            og.at[0, :, main_of(z, dx, c)], a_buf.at[q, pl.ds(0, tok), :], a_loc.at[q]
        )

    def a_remote(z, dx):
        q = z * nx + dx
        return remote(
            og.at[0, :, main_of(z, dx, 1 - c)], a_buf.at[q, pl.ds(tok, tok), :],
            a_snd.at[q], a_rcv.at[q], partner,
        )

    def tail_local(dx):
        return pltpu.make_async_copy(
            og.at[0, :, tail_of(zh, dx, c)], a2.at[dx, pl.ds(0, tok), :], c_loc.at[dx]
        )

    def tail_load(g, dx):
        z = zh if g == 0 else 1 - zh
        core = c if g == 1 else 1 - c
        return pltpu.make_async_copy(
            og.at[0, :, tail_of(z, dx, core)], tbuf.at[g, dx], t_sem.at[g, dx]
        )

    def tail_remote(g, dx):
        return remote(
            tbuf.at[g, dx], a2.at[dx, pl.ds((g + 1) * tok, tok), :],
            c_snd.at[g, dx], c_rcv.at[g, dx], (partner, opposite, diagonal)[g],
        )

    def window_cols(j, width=SW):
        return pl.ds(pl.multiple_of(j * width, width), width)

    def b_load(j):
        return pltpu.make_async_copy(hid.at[0, :, window_cols(j)], hbuf.at[j], l_sem.at[j])

    def b_load_first(j):
        return pltpu.make_async_copy(emb.at[:, window_cols(j)], hbuf.at[j], l_sem.at[j])

    def b_remote(j):
        return remote(
            hbuf.at[j], b_buf.at[j, pl.ds(0, tok), :],
            b_snd.at[j], b_rcv.at[j], following,
        )

    def e_direct(j):
        return remote(
            hbuf.at[j], b2.at[j, pl.ds(0, tok), :], e_snd.at[j], e_rcv.at[j], beside
        )

    def e_relay(j):
        return remote(hbuf.at[j], relay.at[j], e_snd.at[j], k_rcv.at[j], beside)

    def e_pass(j):
        return remote(
            relay.at[j], b2.at[j, pl.ds(0, tok), :], k_snd.at[j], e_rcv.at[j], skipped
        )

    def forward(j):
        return remote(
            b_buf.at[j, pl.ds(0, tok), :], b_buf.at[j, pl.ds(tok, tok), :],
            f_snd.at[j], f_rcv.at[j], partner,
        )

    def forward2(j):
        return remote(
            b2.at[j, pl.ds(0, tok), :], b2.at[j, pl.ds(tok, tok), :],
            h_snd.at[j], h_rcv.at[j], partner,
        )

    def first(d, j, h):
        part = pl.ds(h * SW, SW)
        return remote(
            m1.at[d, j, part, :], r1.at[d, j, part, :],
            m1_snd.at[d, j, h], m1_rcv.at[d, j, h], left if d else right,
        )

    def second(d, z, j):
        return remote(
            m2.at[d, z, j], r2.at[d, z, j], m2_snd.at[d, z, j], m2_rcv.at[d, z, j],
            left if d else right,
        )

    def first2(d, u):
        return remote(
            n1.at[d, u], s1.at[d, u], n1_snd.at[d, u], n1_rcv.at[d, u], left if d else right
        )

    def second2(d, h, u):
        return remote(
            n2.at[d, h, u], s2.at[d, h, u], n2_snd.at[d, h, u], n2_rcv.at[d, h, u],
            left if d else right,
        )

    def last(j):
        return remote(zs.at[j], zr.at[j], z_snd.at[j], z_rcv.at[j], opposite)

    def factor_x(own_z, k):
        z = zh if own_z else 1 - zh
        n = (0 if own_z else nx - 1) + k - 1
        return remote(ag.at[c, z, x], ag.at[c, z, x], g_snd.at[n], g_rcv.at[n], (s, spot(k)))

    def factor_z():
        n = 2 * nx - 2
        return remote(ag.at[c, zh, x], ag.at[c, zh, x], g_snd.at[n], g_rcv.at[n], opposite)

    def factor_c():
        n = 2 * nx - 1
        return remote(ag.at[c], ag.at[c], g_snd.at[n], g_rcv.at[n], partner)

    def store(j):
        return pltpu.make_async_copy(
            obuf.at[j], out.at[0, pl.ds(0, main), window_cols(j, CW)], o_sem.at[j]
        )

    def store2(j):
        return pltpu.make_async_copy(
            obuf2.at[j], out.at[0, pl.ds(main, tail), window_cols(j)], o2_sem.at[j]
        )

    def send_b(j):
        b_remote(j).start()

    def take_b(j):
        b_remote(j).wait_recv()
        forward(j).start()

    def send_b2(j):
        @pl.when(even)
        def _():
            e_direct(j).start()

        @pl.when(jnp.logical_not(even))
        def _():
            e_relay(j).start()

    def pass_b2(j):
        @pl.when(even)
        def _():
            e_relay(j).wait_recv()
            e_pass(j).start()

    def take_b2(j):
        @pl.when(even)
        def _():
            e_pass(j).wait_recv()

        @pl.when(jnp.logical_not(even))
        def _():
            e_direct(j).wait_recv()

        forward2(j).start()

    def wait_a(*pairs):
        for z, dx in pairs:
            a_local(z, dx).wait()
            a_remote(z, dx).wait_recv()

    load_counts = pltpu.make_async_copy(counts_in, counts, i_sem.at[0])
    load_owners = pltpu.make_async_copy(owners_in, owners, i_sem.at[1])
    def load_b(j, carry):
        @pl.when(s == sections - 1)
        def _():
            b_load_first(j).start()

        @pl.when(s < sections - 1)
        def _():
            b_load(j).start()

        return carry

    lax.fori_loop(0, ns, load_b, 0)
    load_counts.start()
    load_owners.start()
    for z, dx in ((0, 2), (1, 2), (1, 1), (0, 3), (0, 1), (1, 3), (0, 0), (1, 0)):
        a_local(z, dx).start()
    for dx in range(nx):
        tail_local(dx).start()
        for g in range(3):
            tail_load(g, dx).start()
    barrier = pltpu.get_barrier_semaphore()
    neighbours = (
        right, left, across, opposite, partner, diagonal, following, previous,
        beside, skipped, skipping,
    )
    for device in neighbours:
        pl.semaphore_signal(barrier, inc=1, device_id=device, device_id_type=MESH)
    ag[c, zh, x] = ainv[0, 0]
    pl.semaphore_wait(barrier, len(neighbours))

    b_load(0).wait()
    send_b(0)
    factor_z().start()
    for z, dx in ((0, 2), (1, 2), (1, 1), (0, 3), (0, 1), (1, 3)):
        a_remote(z, dx).start()
    for k in range(1, nx):
        factor_x(True, k).start()
    send_b2(0)
    for j in range(1, EARLY):
        b_load(j).wait()
        send_b(j)
        send_b2(j)
    load_counts.wait()
    load_owners.wait()
    take_b(0)
    for z, dx in ((0, 0), (1, 0)):
        a_remote(z, dx).start()
    for j in range(EARLY, ns):
        b_load(j).wait()
        if j < AHEAD:
            send_b(j)
        send_b2(j)
    for dx in range(nx):
        tail_load(0, dx).wait()
        tail_remote(0, dx).start()

    def bounds(z, core):
        replica = spot(0, z, core)
        return counts[0, replica], counts[1, replica]

    half = tok // 2

    def transpose(source, target, j, z):
        limits = (*bounds(z, c), *bounds(z, 1 - c))
        for p in range(4):
            piece = source[j, pl.ds(p * half, half), :].astype(F32)
            slots = lax.broadcasted_iota(jnp.int32, piece.shape, 0)
            piece = jnp.where(slots < limits[p], piece, 0.0)
            target[window_cols(j), pl.ds(p * half, half)] = piece.T.astype(BF16)

    def term(j, q):
        return jnp.dot(bt[window_cols(j, CW), :], a_buf[q], preferred_element_type=F32)

    def scale(width):
        total = jnp.int32(0)
        for r in range(counts.shape[0]):
            for m in range(counts.shape[1]):
                total = total + counts[r, m]
        return 1.0 / jnp.sqrt(jnp.full((1, width), total.astype(F32)))

    def choose(t, carry):
        owner = owners[0, t]
        slot = jnp.int32(0)
        for t2 in range(window // size):
            slot = slot + jnp.where((owners[0, t2] == owner) & (t2 < t), 1, 0)
        slot = jnp.minimum(slot, ainv.shape[2] - 1)
        chosen[t] = ag[owner % 2, owner // (2 * nx), (owner // 2) % nx, slot]
        return carry

    def finish(j):
        last(j).wait_recv()
        grad = ((own[j] + zr[j].astype(F32)) * scale(main)).astype(BF16)
        adjusted = jnp.concatenate(
            [
                jnp.dot(grad[:, b * size:(b + 1) * size], ginv[0, b], preferred_element_type=F32)
                for b in range(blocks - 1)
            ],
            axis=1,
        ).astype(BF16)
        for k in range(CW // size):
            piece = jnp.dot(
                chosen[j * (CW // size) + k], adjusted[k * size:(k + 1) * size, :],
                preferred_element_type=F32,
            )
            obuf[j, :, pl.ds(k * size, size)] = piece.T.astype(BF16)
        store(j).start()

    def finish2(u, carry):
        for d in range(2):
            for h in range(2):
                second2(d, h, u).wait_recv()
        weights = scale(tail)
        grad = jnp.concatenate(
            [
                ((own2[u, h] + s2[0, h, u].astype(F32) + s2[1, h, u].astype(F32)) * weights)
                .astype(BF16)
                for h in range(2)
            ],
            axis=0,
        )
        adjusted = jnp.dot(grad, ginv[0, blocks - 1], preferred_element_type=F32).astype(BF16)
        for k in range(uw // size):
            t = u * (uw // size) + k
            piece = jnp.dot(
                chosen[t], adjusted[k * size:(k + 1) * size, :], preferred_element_type=F32
            )
            obuf2[t] = piece.T.astype(BF16)
            store2(t).start()
        return carry

    hw = uw // 2

    def begin2(u, carry):
        cols = pl.ds(pl.multiple_of(u * uw, uw), uw)
        near, far = bt[cols, :], bt2[cols, :]

        def side(start):
            return jnp.concatenate([a2[dx, pl.ds(start, 2 * tok), :] for dx in range(nx)], axis=1)

        value = jnp.dot(near, side(0), preferred_element_type=F32) + jnp.dot(
            far, side(2 * tok), preferred_element_type=F32
        )

        def block(h, dx):
            return value[h * hw:(h + 1) * hw, dx * tail:(dx + 1) * tail]

        for d in range(2):
            n1[d, u] = block(d, 2).astype(BF16)
            first2(d, u).start()
        for d, dx in ((0, 1), (1, nx - 1)):
            comb[d, u] = block(d, dx)
            n2[d, 1 - d, u] = block(1 - d, dx).astype(BF16)
        for h in range(2):
            own2[u, h] = block(h, 0)
        return carry

    def middle2(u, carry):
        for d in range(2):
            second2(d, 1 - d, u).start()
        return carry

    def end2(u, carry):
        for d in range(2):
            first2(d, u).wait_recv()
            n2[d, d, u] = (comb[d, u] + s1[d, u].astype(F32)).astype(BF16)
            second2(d, d, u).start()
        return carry

    def step(i, carry):
        @pl.when((i >= 1) & (i < nc + 1))
        def _():
            j = i - 1

            @pl.when(i == 1)
            def _():
                wait_a((0, 1), (1, 3))

            for d, q in ((0, 1), (1, nx + 3)):
                value = term(j, q)
                for h in range(SUBS):
                    first(d, j, h).wait_recv()
                m2[d, d, j] = (value + r1[d, j].astype(F32)).astype(BF16)
                second(d, d, j).start()

        @pl.when(i == 0)
        def _():
            wait_a((0, 2), (1, 2))
            for h in range(SUBS):
                if h:
                    take_b(h)
                forward(h).wait_recv()
                transpose(b_buf, bt, h, zh)
                for d, q in ((0, 2), (1, nx + 2)):
                    part = bt[pl.ds(h * SW, SW), :]
                    m1[d, 0, pl.ds(h * SW, SW), :] = jnp.dot(
                        part, a_buf[q], preferred_element_type=F32
                    ).astype(BF16)
                    first(d, 0, h).start()

        @pl.when((i > 0) & (i < nc))
        def _():
            for h in range(SUBS):
                take_b(i * SUBS + h)
            for h in range(SUBS):
                forward(i * SUBS + h).wait_recv()
                transpose(b_buf, bt, i * SUBS + h, zh)
            for d, q in ((0, 2), (1, nx + 2)):
                m1[d, i] = term(i, q).astype(BF16)
                for h in range(SUBS):
                    first(d, i, h).start()

        @pl.when(i < nc)
        def _():
            @pl.when(i == 0)
            def _():
                wait_a((1, 1), (0, 3))

            for d, q in ((0, nx + 1), (1, 3)):
                m2[d, 1 - d, i] = term(i, q).astype(BF16)
                second(d, 1 - d, i).start()

        @pl.when(i * SUBS + AHEAD < ns)
        def _():
            for h in range(SUBS):
                send_b(i * SUBS + AHEAD + h)

        pieces = [(g, dx) for g in (1, 2) for dx in range(nx)]
        for n, count in enumerate(PACE):
            @pl.when(i == n)
            def _():
                for g, dx in pieces[sum(PACE[:n]):sum(PACE[:n]) + count]:
                    tail_load(g, dx).wait()
                    tail_remote(g, dx).start()

        @pl.when(i == 2)
        def _():
            factor_z().wait_recv()
            for k in range(1, nx):
                factor_x(False, k).start()

        @pl.when(i == 3)
        def _():
            for k in range(1, nx):
                factor_x(True, k).wait_recv()
                factor_x(False, k).wait_recv()
            factor_c().start()

        for n, (low, high) in enumerate(PIECES2):
            @pl.when(i == n + 3)
            def _():
                for j in range(low, high):
                    forward2(j).wait_recv()
                    transpose(b2, bt2, j, 1 - zh)

        @pl.when(i == nc)
        def _():
            for dx in range(nx):
                tail_local(dx).wait()
                for g in range(3):
                    tail_remote(g, dx).wait_recv()
            lax.fori_loop(0, nu, begin2, 0)
            lax.fori_loop(0, nu, middle2, 0)

        @pl.when(i >= 2)
        def _():
            j = i - 2

            @pl.when(i == 2)
            def _():
                wait_a((0, 0), (1, 0))

            away = term(j, (1 - zh) * nx)
            mine = term(j, zh * nx)
            second(0, 1, j).wait_recv()
            second(1, 0, j).wait_recv()
            second(0, 0, j).wait_recv()
            second(1, 1, j).wait_recv()
            zs[j] = (
                away + r2[0, 1 - zh, j].astype(F32) + r2[1, 1 - zh, j].astype(F32)
            ).astype(BF16)
            last(j).start()
            own[j] = mine + r2[0, zh, j].astype(F32) + r2[1, zh, j].astype(F32)

        @pl.when(i == nc + 1)
        def _():
            lax.fori_loop(0, nu, end2, 0)

        for n, (low, high) in enumerate(PIECES2):
            @pl.when(i == n + 1)
            def _():
                for j in range(low, high):
                    pass_b2(j)

            @pl.when(i == n + 2)
            def _():
                for j in range(low, high):
                    take_b2(j)

        @pl.when(i == 2 + LAG)
        def _():
            factor_c().wait_recv()
            lax.fori_loop(0, window // size, choose, 0)

        @pl.when(i >= 2 + LAG)
        def _():
            finish(i - 2 - LAG)

        return carry

    lax.fori_loop(0, nc + 2, step, 0)

    def drain(j, carry):
        b_remote(j).wait_send()

        @pl.when(even)
        def _():
            e_direct(j).wait_send()
            e_pass(j).wait_send()

        @pl.when(jnp.logical_not(even))
        def _():
            e_relay(j).wait_send()

        forward(j).wait_send()
        forward2(j).wait_send()
        return carry

    def drain1(j, carry):
        for d in range(2):
            for h in range(SUBS):
                first(d, j, h).wait_send()
            for z in range(2):
                second(d, z, j).wait_send()
        return carry

    def drain2(u, carry):
        for d in range(2):
            first2(d, u).wait_send()
            for h in range(2):
                second2(d, h, u).wait_send()
        return carry

    def drain3(j, carry):
        last(j).wait_send()
        store(j).wait()
        for h in range(SUBS):
            store2(j * SUBS + h).wait()
        return carry

    def rest(j, carry):
        finish(j)
        return carry

    lax.fori_loop(nc - LAG, nc - 1, rest, 0)
    for dx in range(nx):
        for z in range(2):
            a_remote(z, dx).wait_send()
        for g in range(3):
            tail_remote(g, dx).wait_send()
    for k in range(1, nx):
        factor_x(True, k).wait_send()
        factor_x(False, k).wait_send()
    factor_z().wait_send()
    factor_c().wait_send()
    lax.fori_loop(0, ns, drain, 0)
    lax.fori_loop(0, nc, drain1, 0)
    finish(nc - 1)
    lax.fori_loop(0, nu, finish2, 0)
    lax.fori_loop(0, nu, drain2, 0)
    lax.fori_loop(0, nc, drain3, 0)


def local(sections, groups, embedded, hidden_out, out_grads, counts, owners, ginv, ainv):
    tok, window = embedded.shape
    rows = out_grads.shape[-1] // groups
    size = ginv.shape[-1]
    main = rows - size
    nx = groups // 4
    nc, ns, nu = window // CW, window // SW, window // UW
    hw = UW // 2
    dims = (sections, nx, rows, tok, window)
    hbm = pl.BlockSpec(memory_space=pl.ANY)
    vmem = pl.BlockSpec(memory_space=pltpu.VMEM)
    dma = pltpu.SemaphoreType.DMA
    flops = 2 * tok * out_grads.shape[-1] * window
    return pl.pallas_call(
        functools.partial(kernel, dims),
        out_shape=jax.ShapeDtypeStruct((1, rows, window), BF16),
        in_specs=[hbm, hbm, hbm, hbm, hbm, vmem, vmem],
        out_specs=hbm,
        scratch_shapes=[
            pltpu.SMEM(counts.shape[::-1], jnp.int32),
            pltpu.SMEM(owners.shape[:2], jnp.int32),
            pltpu.VMEM((2 * nx, 2 * tok, main), BF16),
            pltpu.VMEM((nx, 4 * tok, size), BF16),
            pltpu.VMEM((ns, 2 * tok, SW), BF16),
            pltpu.VMEM((ns, 2 * tok, SW), BF16),
            pltpu.VMEM((window, 2 * tok), BF16),
            pltpu.VMEM((window, 2 * tok), BF16),
            pltpu.VMEM((2, nc, CW, main), BF16),
            pltpu.VMEM((2, nc, CW, main), BF16),
            pltpu.VMEM((2, 2, nc, CW, main), BF16),
            pltpu.VMEM((2, 2, nc, CW, main), BF16),
            pltpu.VMEM((nc, CW, main), F32),
            pltpu.VMEM((nc, CW, main), BF16),
            pltpu.VMEM((nc, CW, main), BF16),
            pltpu.VMEM((2, nu, hw, size), BF16),
            pltpu.VMEM((2, nu, hw, size), BF16),
            pltpu.VMEM((2, 2, nu, hw, size), BF16),
            pltpu.VMEM((2, 2, nu, hw, size), BF16),
            pltpu.VMEM((2, nu, hw, size), F32),
            pltpu.VMEM((nu, 2, hw, size), F32),
            pltpu.VMEM((2, 2, nx) + ainv.shape[2:], BF16),
            pltpu.VMEM((window // size, size, size), BF16),
            pltpu.VMEM((nc, main, CW), BF16),
            pltpu.VMEM((ns, size, SW), BF16),
            pltpu.VMEM((ns, tok, SW), BF16),
            pltpu.VMEM((3, nx, tok, size), BF16),
            pltpu.VMEM((ns, tok, SW), BF16),
            dma((2,)), dma((ns,)), dma((3, nx)), dma((ns,)), dma((ns,)), dma((2 * nx,)), dma((2 * nx,)), dma((2 * nx,)),
            dma((nx,)), dma((3, nx)), dma((3, nx)),
            dma((ns,)), dma((ns,)), dma((ns,)), dma((ns,)), dma((ns,)), dma((ns,)),
            dma((ns,)), dma((ns,)),
            dma((2, nc, SUBS)), dma((2, nc, SUBS)), dma((2, 2, nc)), dma((2, 2, nc)),
            dma((2, nu)), dma((2, nu)), dma((2, 2, nu)), dma((2, 2, nu)),
            dma((nc,)), dma((nc,)), dma((2 * nx,)), dma((2 * nx,)), dma((nc,)), dma((ns,)),
        ],
        compiler_params=pltpu.CompilerParams(
            collective_id=0, has_side_effects=True, vmem_limit_bytes=60 << 20
        ),
        cost_estimate=pl.CostEstimate(
            flops=flops, bytes_accessed=2 * out_grads.size, transcendentals=0
        ),
    )(embedded, hidden_out, out_grads, counts.T, owners[:, :, 0], ginv, ainv)


def solution(mesh):
    placed = (
        P("dp", None),
        P("section", "dp", None),
        P("section", "dp", None),
        P(),
        P("section", None, None),
        P("section", "dp", None, None),
        P("section", "dp", None, None, None),
    )
    return jax.shard_map(
        functools.partial(local, mesh.shape["section"], mesh.shape["dp"]),
        mesh=mesh, in_specs=placed, out_specs=P("section", "dp", None), check_vma=False,
    )
```

```python
import functools

import jax
import jax.numpy as jnp
from jax import lax
from jax.experimental import pallas as pl
from jax.experimental.pallas import tpu as pltpu
from jax.sharding import PartitionSpec as P

MESH = pl.DeviceIdType.MESH
F32 = jnp.float32
BF16 = jnp.bfloat16

SW = 128
SUBS = 2
CW = SUBS * SW
UW = 512
AHEAD = 4
EARLY = 4
PIECES2 = ((0, 2), (2, 6), (6, 10), (10, 12))
LAG = 2
PACE = (2, 2, 1, 1, 1, 1)


def kernel(
    dims, emb, hid, og, counts_in, owners_in, ginv, ainv, out,
    counts, owners, a_buf, a2, b_buf, b2, bt, bt2, m1, r1, m2, r2, own, zs, zr,
    n1, s1, n2, s2, comb, own2, ag, chosen, obuf, obuf2, hbuf, tbuf, relay,
    i_sem, l_sem, t_sem, k_snd, k_rcv, a_loc, a_snd, a_rcv, c_loc, c_snd, c_rcv, b_snd, b_rcv, e_snd, e_rcv, f_snd, f_rcv,
    h_snd, h_rcv, m1_snd, m1_rcv, m2_snd, m2_rcv, n1_snd, n1_rcv, n2_snd, n2_rcv,
    z_snd, z_rcv, g_snd, g_rcv, o_sem, o2_sem,
):
    sections, nx, rows, tok, window = dims
    nc = window // CW
    ns = window // SW
    nu = window // UW
    uw = UW
    size = ginv.shape[-1]
    blocks = ginv.shape[1]
    tail = size
    main = rows - tail
    s = lax.axis_index("section")
    dp = lax.axis_index("dp")
    zh, x, c = dp // (2 * nx), (dp // 2) % nx, dp % 2

    def spot(dx=0, z=None, core=None):
        z = zh if z is None else z
        core = c if core is None else core
        return (z * nx + (x + dx) % nx) * 2 + core

    right, left, across = (s, spot(1)), (s, spot(nx - 1)), (s, spot(2))
    opposite, partner = (s, spot(z=1 - zh)), (s, spot(core=1 - c))
    diagonal = (s, spot(z=1 - zh, core=1 - c))
    following, previous = ((s + 1) % sections, dp), ((s + sections - 1) % sections, dp)
    even = s % 2 == 0
    beside = (s // 2 * 2 + 1 - s % 2, opposite[1])
    skipped, skipping = ((s + 2) % sections, dp), ((s + sections - 2) % sections, dp)

    def remote(src, dst, snd, rcv, device):
        return pltpu.make_async_remote_copy(
            src_ref=src, dst_ref=dst, send_sem=snd, recv_sem=rcv,
            device_id=device, device_id_type=MESH,
        )

    def main_of(z, dx, core):
        return pl.ds(pl.multiple_of(spot(dx, z, core) * rows, rows), main)

    def tail_of(z, dx, core):
        return pl.ds(pl.multiple_of(spot(dx, z, core) * rows + main, tail), tail)

    def a_local(z, dx):
        q = z * nx + dx
        return pltpu.make_async_copy(
            og.at[0, :, main_of(z, dx, c)], a_buf.at[q, pl.ds(0, tok), :], a_loc.at[q]
        )

    def a_remote(z, dx):
        q = z * nx + dx
        return remote(
            og.at[0, :, main_of(z, dx, 1 - c)], a_buf.at[q, pl.ds(tok, tok), :],
            a_snd.at[q], a_rcv.at[q], partner,
        )

    def tail_local(dx):
        return pltpu.make_async_copy(
            og.at[0, :, tail_of(zh, dx, c)], a2.at[dx, pl.ds(0, tok), :], c_loc.at[dx]
        )

    def tail_load(g, dx):
        z = zh if g == 0 else 1 - zh
        core = c if g == 1 else 1 - c
        return pltpu.make_async_copy(
            og.at[0, :, tail_of(z, dx, core)], tbuf.at[g, dx], t_sem.at[g, dx]
        )

    def tail_remote(g, dx):
        return remote(
            tbuf.at[g, dx], a2.at[dx, pl.ds((g + 1) * tok, tok), :],
            c_snd.at[g, dx], c_rcv.at[g, dx], (partner, opposite, diagonal)[g],
        )

    def window_cols(j, width=SW):
        return pl.ds(pl.multiple_of(j * width, width), width)

    def b_load(j):
        return pltpu.make_async_copy(hid.at[0, :, window_cols(j)], hbuf.at[j], l_sem.at[j])

    def b_load_first(j):
        return pltpu.make_async_copy(emb.at[:, window_cols(j)], hbuf.at[j], l_sem.at[j])

    def b_remote(j):
        return remote(
            hbuf.at[j], b_buf.at[j, pl.ds(0, tok), :],
            b_snd.at[j], b_rcv.at[j], following,
        )

    def e_direct(j):
        return remote(
            hbuf.at[j], b2.at[j, pl.ds(0, tok), :], e_snd.at[j], e_rcv.at[j], beside
        )

    def e_relay(j):
        return remote(hbuf.at[j], relay.at[j], e_snd.at[j], k_rcv.at[j], beside)

    def e_pass(j):
        return remote(
            relay.at[j], b2.at[j, pl.ds(0, tok), :], k_snd.at[j], e_rcv.at[j], skipped
        )

    def forward(j):
        return remote(
            b_buf.at[j, pl.ds(0, tok), :], b_buf.at[j, pl.ds(tok, tok), :],
            f_snd.at[j], f_rcv.at[j], partner,
        )

    def forward2(j):
        return remote(
            b2.at[j, pl.ds(0, tok), :], b2.at[j, pl.ds(tok, tok), :],
            h_snd.at[j], h_rcv.at[j], partner,
        )

    def first(d, j, h):
        part = pl.ds(h * SW, SW)
        return remote(
            m1.at[d, j, part, :], r1.at[d, j, part, :],
            m1_snd.at[d, j, h], m1_rcv.at[d, j, h], left if d else right,
        )

    def second(d, z, j):
        return remote(
            m2.at[d, z, j], r2.at[d, z, j], m2_snd.at[d, z, j], m2_rcv.at[d, z, j],
            left if d else right,
        )

    def first2(d, u):
        return remote(
            n1.at[d, u], s1.at[d, u], n1_snd.at[d, u], n1_rcv.at[d, u], left if d else right
        )

    def second2(d, h, u):
        return remote(
            n2.at[d, h, u], s2.at[d, h, u], n2_snd.at[d, h, u], n2_rcv.at[d, h, u],
            left if d else right,
        )

    def last(j):
        return remote(zs.at[j], zr.at[j], z_snd.at[j], z_rcv.at[j], opposite)

    def factor_x(k):
        n = k - 1
        return remote(ag.at[c, zh, x], ag.at[c, zh, x], g_snd.at[n], g_rcv.at[n], (s, spot(k)))

    def factor_z():
        n = nx - 1
        return remote(ag.at[c, zh], ag.at[c, zh], g_snd.at[n], g_rcv.at[n], opposite)

    def factor_c():
        n = nx
        return remote(ag.at[c], ag.at[c], g_snd.at[n], g_rcv.at[n], partner)

    def store(j):
        return pltpu.make_async_copy(
            obuf.at[j], out.at[0, pl.ds(0, main), window_cols(j, CW)], o_sem.at[j]
        )

    def store2(j):
        return pltpu.make_async_copy(
            obuf2.at[j], out.at[0, pl.ds(main, tail), window_cols(j)], o2_sem.at[j]
        )

    def send_b(j):
        b_remote(j).start()

    def take_b(j):
        b_remote(j).wait_recv()
        forward(j).start()

    def send_b2(j):
        @pl.when(even)
        def _():
            e_direct(j).start()

        @pl.when(jnp.logical_not(even))
        def _():
            e_relay(j).start()

    def pass_b2(j):
        @pl.when(even)
        def _():
            e_relay(j).wait_recv()
            e_pass(j).start()

    def take_b2(j):
        @pl.when(even)
        def _():
            e_pass(j).wait_recv()

        @pl.when(jnp.logical_not(even))
        def _():
            e_direct(j).wait_recv()

        forward2(j).start()

    def wait_a(*pairs):
        for z, dx in pairs:
            a_local(z, dx).wait()
            a_remote(z, dx).wait_recv()

    load_counts = pltpu.make_async_copy(counts_in, counts, i_sem.at[0])
    load_owners = pltpu.make_async_copy(owners_in, owners, i_sem.at[1])
    def load_b(j, carry):
        @pl.when(s == sections - 1)
        def _():
            b_load_first(j).start()

        @pl.when(s < sections - 1)
        def _():
            b_load(j).start()

        return carry

    lax.fori_loop(0, ns, load_b, 0)
    load_counts.start()
    load_owners.start()
    for z, dx in ((0, 2), (1, 2), (1, 1), (0, 3), (0, 1), (1, 3), (0, 0), (1, 0)):
        a_local(z, dx).start()
    for dx in range(nx):
        tail_local(dx).start()
        for g in range(3):
            tail_load(g, dx).start()
    barrier = pltpu.get_barrier_semaphore()
    neighbours = (
        right, left, across, opposite, partner, diagonal, following, previous,
        beside, skipped, skipping,
    )
    for device in neighbours:
        pl.semaphore_signal(barrier, inc=1, device_id=device, device_id_type=MESH)
    ag[c, zh, x] = ainv[0, 0]
    pl.semaphore_wait(barrier, len(neighbours))

    b_load(0).wait()
    send_b(0)
    for z, dx in ((0, 2), (1, 2), (1, 1), (0, 3), (0, 1), (1, 3)):
        a_remote(z, dx).start()
    for k in range(1, nx):
        factor_x(k).start()
    send_b2(0)
    for j in range(1, EARLY):
        b_load(j).wait()
        send_b(j)
        send_b2(j)
    load_counts.wait()
    load_owners.wait()
    take_b(0)
    for z, dx in ((0, 0), (1, 0)):
        a_remote(z, dx).start()
    for j in range(EARLY, ns):
        b_load(j).wait()
        if j < AHEAD:
            send_b(j)
        send_b2(j)
    for dx in range(nx):
        tail_load(0, dx).wait()
        tail_remote(0, dx).start()

    def bounds(z, core):
        replica = spot(0, z, core)
        return counts[0, replica], counts[1, replica]

    half = tok // 2

    def transpose(source, target, j, z):
        limits = (*bounds(z, c), *bounds(z, 1 - c))
        for p in range(4):
            piece = source[j, pl.ds(p * half, half), :].astype(F32)
            slots = lax.broadcasted_iota(jnp.int32, piece.shape, 0)
            piece = jnp.where(slots < limits[p], piece, 0.0)
            target[window_cols(j), pl.ds(p * half, half)] = piece.T.astype(BF16)

    def term(j, q):
        return jnp.dot(bt[window_cols(j, CW), :], a_buf[q], preferred_element_type=F32)

    def scale(width):
        total = jnp.int32(0)
        for r in range(counts.shape[0]):
            for m in range(counts.shape[1]):
                total = total + counts[r, m]
        return 1.0 / jnp.sqrt(jnp.full((1, width), total.astype(F32)))

    def choose(t, carry):
        owner = owners[0, t]
        slot = jnp.int32(0)
        for t2 in range(window // size):
            slot = slot + jnp.where((owners[0, t2] == owner) & (t2 < t), 1, 0)
        slot = jnp.minimum(slot, ainv.shape[2] - 1)
        chosen[t] = ag[owner % 2, owner // (2 * nx), (owner // 2) % nx, slot]
        return carry

    def finish(j):
        last(j).wait_recv()
        grad = ((own[j] + zr[j].astype(F32)) * scale(main)).astype(BF16)
        adjusted = jnp.concatenate(
            [
                jnp.dot(grad[:, b * size:(b + 1) * size], ginv[0, b], preferred_element_type=F32)
                for b in range(blocks - 1)
            ],
            axis=1,
        ).astype(BF16)
        for k in range(CW // size):
            piece = jnp.dot(
                chosen[j * (CW // size) + k], adjusted[k * size:(k + 1) * size, :],
                preferred_element_type=F32,
            )
            obuf[j, :, pl.ds(k * size, size)] = piece.T.astype(BF16)
        store(j).start()

    def finish2(u, carry):
        for d in range(2):
            for h in range(2):
                second2(d, h, u).wait_recv()
        weights = scale(tail)
        grad = jnp.concatenate(
            [
                ((own2[u, h] + s2[0, h, u].astype(F32) + s2[1, h, u].astype(F32)) * weights)
                .astype(BF16)
                for h in range(2)
            ],
            axis=0,
        )
        adjusted = jnp.dot(grad, ginv[0, blocks - 1], preferred_element_type=F32).astype(BF16)
        for k in range(uw // size):
            t = u * (uw // size) + k
            piece = jnp.dot(
                chosen[t], adjusted[k * size:(k + 1) * size, :], preferred_element_type=F32
            )
            obuf2[t] = piece.T.astype(BF16)
            store2(t).start()
        return carry

    hw = uw // 2

    def begin2(u, carry):
        cols = pl.ds(pl.multiple_of(u * uw, uw), uw)
        near, far = bt[cols, :], bt2[cols, :]

        def side(start):
            return jnp.concatenate([a2[dx, pl.ds(start, 2 * tok), :] for dx in range(nx)], axis=1)

        value = jnp.dot(near, side(0), preferred_element_type=F32) + jnp.dot(
            far, side(2 * tok), preferred_element_type=F32
        )

        def block(h, dx):
            return value[h * hw:(h + 1) * hw, dx * tail:(dx + 1) * tail]

        for d in range(2):
            n1[d, u] = block(d, 2).astype(BF16)
            first2(d, u).start()
        for d, dx in ((0, 1), (1, nx - 1)):
            comb[d, u] = block(d, dx)
            n2[d, 1 - d, u] = block(1 - d, dx).astype(BF16)
        for h in range(2):
            own2[u, h] = block(h, 0)
        return carry

    def middle2(u, carry):
        for d in range(2):
            second2(d, 1 - d, u).start()
        return carry

    def end2(u, carry):
        for d in range(2):
            first2(d, u).wait_recv()
            n2[d, d, u] = (comb[d, u] + s1[d, u].astype(F32)).astype(BF16)
            second2(d, d, u).start()
        return carry

    def step(i, carry):
        @pl.when((i >= 1) & (i < nc + 1))
        def _():
            j = i - 1

            @pl.when(i == 1)
            def _():
                wait_a((0, 1), (1, 3))

            for d, q in ((0, 1), (1, nx + 3)):
                value = term(j, q)
                for h in range(SUBS):
                    first(d, j, h).wait_recv()
                m2[d, d, j] = (value + r1[d, j].astype(F32)).astype(BF16)
                second(d, d, j).start()

        @pl.when(i == 0)
        def _():
            wait_a((0, 2), (1, 2))
            for h in range(SUBS):
                if h:
                    take_b(h)
                forward(h).wait_recv()
                transpose(b_buf, bt, h, zh)
                for d, q in ((0, 2), (1, nx + 2)):
                    part = bt[pl.ds(h * SW, SW), :]
                    m1[d, 0, pl.ds(h * SW, SW), :] = jnp.dot(
                        part, a_buf[q], preferred_element_type=F32
                    ).astype(BF16)
                    first(d, 0, h).start()

        @pl.when((i > 0) & (i < nc))
        def _():
            for h in range(SUBS):
                take_b(i * SUBS + h)
            for h in range(SUBS):
                forward(i * SUBS + h).wait_recv()
                transpose(b_buf, bt, i * SUBS + h, zh)
            for d, q in ((0, 2), (1, nx + 2)):
                m1[d, i] = term(i, q).astype(BF16)
                for h in range(SUBS):
                    first(d, i, h).start()

        @pl.when(i < nc)
        def _():
            @pl.when(i == 0)
            def _():
                wait_a((1, 1), (0, 3))

            for d, q in ((0, nx + 1), (1, 3)):
                m2[d, 1 - d, i] = term(i, q).astype(BF16)
                second(d, 1 - d, i).start()

        @pl.when(i * SUBS + AHEAD < ns)
        def _():
            for h in range(SUBS):
                send_b(i * SUBS + AHEAD + h)

        pieces = [(g, dx) for g in (1, 2) for dx in range(nx)]
        for n, count in enumerate(PACE):
            @pl.when(i == n)
            def _():
                for g, dx in pieces[sum(PACE[:n]):sum(PACE[:n]) + count]:
                    tail_load(g, dx).wait()
                    tail_remote(g, dx).start()

        @pl.when(i == 1)
        def _():
            for k in range(1, nx):
                factor_x(k).wait_recv()
            factor_z().start()

        @pl.when(i == 1 + LAG)
        def _():
            factor_z().wait_recv()
            factor_c().start()

        for n, (low, high) in enumerate(PIECES2):
            @pl.when(i == n + 3)
            def _():
                for j in range(low, high):
                    forward2(j).wait_recv()
                    transpose(b2, bt2, j, 1 - zh)

        @pl.when(i == nc)
        def _():
            for dx in range(nx):
                tail_local(dx).wait()
                for g in range(3):
                    tail_remote(g, dx).wait_recv()
            lax.fori_loop(0, nu, begin2, 0)
            lax.fori_loop(0, nu, middle2, 0)

        @pl.when(i >= 2)
        def _():
            j = i - 2

            @pl.when(i == 2)
            def _():
                wait_a((0, 0), (1, 0))

            away = term(j, (1 - zh) * nx)
            mine = term(j, zh * nx)
            second(0, 1, j).wait_recv()
            second(1, 0, j).wait_recv()
            second(0, 0, j).wait_recv()
            second(1, 1, j).wait_recv()
            zs[j] = (
                away + r2[0, 1 - zh, j].astype(F32) + r2[1, 1 - zh, j].astype(F32)
            ).astype(BF16)
            last(j).start()
            own[j] = mine + r2[0, zh, j].astype(F32) + r2[1, zh, j].astype(F32)

        @pl.when(i == nc + 1)
        def _():
            lax.fori_loop(0, nu, end2, 0)

        for n, (low, high) in enumerate(PIECES2):
            @pl.when(i == n + 1)
            def _():
                for j in range(low, high):
                    pass_b2(j)

            @pl.when(i == n + 2)
            def _():
                for j in range(low, high):
                    take_b2(j)

        @pl.when(i == 2 + LAG)
        def _():
            factor_c().wait_recv()
            lax.fori_loop(0, window // size, choose, 0)

        @pl.when(i >= 2 + LAG)
        def _():
            finish(i - 2 - LAG)

        return carry

    lax.fori_loop(0, nc + 2, step, 0)

    def drain(j, carry):
        b_remote(j).wait_send()

        @pl.when(even)
        def _():
            e_direct(j).wait_send()
            e_pass(j).wait_send()

        @pl.when(jnp.logical_not(even))
        def _():
            e_relay(j).wait_send()

        forward(j).wait_send()
        forward2(j).wait_send()
        return carry

    def drain1(j, carry):
        for d in range(2):
            for h in range(SUBS):
                first(d, j, h).wait_send()
            for z in range(2):
                second(d, z, j).wait_send()
        return carry

    def drain2(u, carry):
        for d in range(2):
            first2(d, u).wait_send()
            for h in range(2):
                second2(d, h, u).wait_send()
        return carry

    def drain3(j, carry):
        last(j).wait_send()
        store(j).wait()
        for h in range(SUBS):
            store2(j * SUBS + h).wait()
        return carry

    def rest(j, carry):
        finish(j)
        return carry

    lax.fori_loop(nc - LAG, nc - 1, rest, 0)
    for dx in range(nx):
        for z in range(2):
            a_remote(z, dx).wait_send()
        for g in range(3):
            tail_remote(g, dx).wait_send()
    for k in range(1, nx):
        factor_x(k).wait_send()
    factor_z().wait_send()
    factor_c().wait_send()
    lax.fori_loop(0, ns, drain, 0)
    lax.fori_loop(0, nc, drain1, 0)
    finish(nc - 1)
    lax.fori_loop(0, nu, finish2, 0)
    lax.fori_loop(0, nu, drain2, 0)
    lax.fori_loop(0, nc, drain3, 0)


def local(sections, groups, embedded, hidden_out, out_grads, counts, owners, ginv, ainv):
    tok, window = embedded.shape
    rows = out_grads.shape[-1] // groups
    size = ginv.shape[-1]
    main = rows - size
    nx = groups // 4
    nc, ns, nu = window // CW, window // SW, window // UW
    hw = UW // 2
    dims = (sections, nx, rows, tok, window)
    hbm = pl.BlockSpec(memory_space=pl.ANY)
    vmem = pl.BlockSpec(memory_space=pltpu.VMEM)
    dma = pltpu.SemaphoreType.DMA
    flops = 2 * tok * out_grads.shape[-1] * window
    return pl.pallas_call(
        functools.partial(kernel, dims),
        out_shape=jax.ShapeDtypeStruct((1, rows, window), BF16),
        in_specs=[hbm, hbm, hbm, hbm, hbm, vmem, vmem],
        out_specs=hbm,
        scratch_shapes=[
            pltpu.SMEM(counts.shape[::-1], jnp.int32),
            pltpu.SMEM(owners.shape[:2], jnp.int32),
            pltpu.VMEM((2 * nx, 2 * tok, main), BF16),
            pltpu.VMEM((nx, 4 * tok, size), BF16),
            pltpu.VMEM((ns, 2 * tok, SW), BF16),
            pltpu.VMEM((ns, 2 * tok, SW), BF16),
            pltpu.VMEM((window, 2 * tok), BF16),
            pltpu.VMEM((window, 2 * tok), BF16),
            pltpu.VMEM((2, nc, CW, main), BF16),
            pltpu.VMEM((2, nc, CW, main), BF16),
            pltpu.VMEM((2, 2, nc, CW, main), BF16),
            pltpu.VMEM((2, 2, nc, CW, main), BF16),
            pltpu.VMEM((nc, CW, main), F32),
            pltpu.VMEM((nc, CW, main), BF16),
            pltpu.VMEM((nc, CW, main), BF16),
            pltpu.VMEM((2, nu, hw, size), BF16),
            pltpu.VMEM((2, nu, hw, size), BF16),
            pltpu.VMEM((2, 2, nu, hw, size), BF16),
            pltpu.VMEM((2, 2, nu, hw, size), BF16),
            pltpu.VMEM((2, nu, hw, size), F32),
            pltpu.VMEM((nu, 2, hw, size), F32),
            pltpu.VMEM((2, 2, nx) + ainv.shape[2:], BF16),
            pltpu.VMEM((window // size, size, size), BF16),
            pltpu.VMEM((nc, main, CW), BF16),
            pltpu.VMEM((ns, size, SW), BF16),
            pltpu.VMEM((ns, tok, SW), BF16),
            pltpu.VMEM((3, nx, tok, size), BF16),
            pltpu.VMEM((ns, tok, SW), BF16),
            dma((2,)), dma((ns,)), dma((3, nx)), dma((ns,)), dma((ns,)), dma((2 * nx,)), dma((2 * nx,)), dma((2 * nx,)),
            dma((nx,)), dma((3, nx)), dma((3, nx)),
            dma((ns,)), dma((ns,)), dma((ns,)), dma((ns,)), dma((ns,)), dma((ns,)),
            dma((ns,)), dma((ns,)),
            dma((2, nc, SUBS)), dma((2, nc, SUBS)), dma((2, 2, nc)), dma((2, 2, nc)),
            dma((2, nu)), dma((2, nu)), dma((2, 2, nu)), dma((2, 2, nu)),
            dma((nc,)), dma((nc,)), dma((nx + 1,)), dma((nx + 1,)), dma((nc,)), dma((ns,)),
        ],
        compiler_params=pltpu.CompilerParams(
            collective_id=0, has_side_effects=True, vmem_limit_bytes=60 << 20
        ),
        cost_estimate=pl.CostEstimate(
            flops=flops, bytes_accessed=2 * out_grads.size, transcendentals=0
        ),
    )(embedded, hidden_out, out_grads, counts.T, owners[:, :, 0], ginv, ainv)


def solution(mesh):
    placed = (
        P("dp", None),
        P("section", "dp", None),
        P("section", "dp", None),
        P(),
        P("section", None, None),
        P("section", "dp", None, None),
        P("section", "dp", None, None, None),
    )
    return jax.shard_map(
        functools.partial(local, mesh.shape["section"], mesh.shape["dp"]),
        mesh=mesh, in_specs=placed, out_specs=P("section", "dp", None), check_vma=False,
    )
```

```python
import functools

import jax
import jax.numpy as jnp
from jax import lax
from jax.experimental import pallas as pl
from jax.experimental.pallas import tpu as pltpu
from jax.sharding import PartitionSpec as P

MESH = pl.DeviceIdType.MESH
F32 = jnp.float32
BF16 = jnp.bfloat16

SW = 128
SUBS = 2
CW = SUBS * SW
UW = 512
AHEAD = 4
EARLY = 4
PIECES2 = ((0, 2), (2, 6), (6, 10), (10, 12))
LAG = 2
PACE = (2, 2, 1, 1, 1, 1)


def kernel(
    dims, emb, hid, og, counts_in, owners_in, ginv, ainv, out,
    counts, owners, a_buf, a2, b_buf, b2, bt, bt2, m1, r1, m2, r2, own, zs, zr,
    n1, s1, n2, s2, comb, own2, ag, chosen, obuf, obuf2, hbuf, tbuf, relay,
    i_sem, l_sem, t_sem, k_snd, k_rcv, a_loc, a_snd, a_rcv, c_loc, c_snd, c_rcv, b_snd, b_rcv, e_snd, e_rcv, f_snd, f_rcv,
    h_snd, h_rcv, m1_snd, m1_rcv, m2_snd, m2_rcv, n1_snd, n1_rcv, n2_snd, n2_rcv,
    z_snd, z_rcv, g_snd, g_rcv, o_sem, o2_sem,
):
    sections, nx, rows, tok, window = dims
    nc = window // CW
    ns = window // SW
    nu = window // UW
    uw = UW
    size = ginv.shape[-1]
    blocks = ginv.shape[1]
    tail = size
    main = rows - tail
    s = lax.axis_index("section")
    dp = lax.axis_index("dp")
    zh, x, c = dp // (2 * nx), (dp // 2) % nx, dp % 2

    def spot(dx=0, z=None, core=None):
        z = zh if z is None else z
        core = c if core is None else core
        return (z * nx + (x + dx) % nx) * 2 + core

    right, left, across = (s, spot(1)), (s, spot(nx - 1)), (s, spot(2))
    opposite, partner = (s, spot(z=1 - zh)), (s, spot(core=1 - c))
    diagonal = (s, spot(z=1 - zh, core=1 - c))
    following, previous = ((s + 1) % sections, dp), ((s + sections - 1) % sections, dp)
    even = s % 2 == 0
    beside = (s // 2 * 2 + 1 - s % 2, opposite[1])
    skipped, skipping = ((s + 2) % sections, dp), ((s + sections - 2) % sections, dp)

    def remote(src, dst, snd, rcv, device):
        return pltpu.make_async_remote_copy(
            src_ref=src, dst_ref=dst, send_sem=snd, recv_sem=rcv,
            device_id=device, device_id_type=MESH,
        )

    def main_of(z, dx, core):
        return pl.ds(pl.multiple_of(spot(dx, z, core) * rows, rows), main)

    def tail_of(z, dx, core):
        return pl.ds(pl.multiple_of(spot(dx, z, core) * rows + main, tail), tail)

    def a_local(z, dx):
        q = z * nx + dx
        return pltpu.make_async_copy(
            og.at[0, :, main_of(z, dx, c)], a_buf.at[q, pl.ds(0, tok), :], a_loc.at[q]
        )

    def a_remote(z, dx):
        q = z * nx + dx
        return remote(
            og.at[0, :, main_of(z, dx, 1 - c)], a_buf.at[q, pl.ds(tok, tok), :],
            a_snd.at[q], a_rcv.at[q], partner,
        )

    def tail_local(dx):
        return pltpu.make_async_copy(
            og.at[0, :, tail_of(zh, dx, c)], a2.at[dx, pl.ds(0, tok), :], c_loc.at[dx]
        )

    def tail_load(g, dx):
        z = zh if g == 0 else 1 - zh
        core = c if g == 1 else 1 - c
        return pltpu.make_async_copy(
            og.at[0, :, tail_of(z, dx, core)], tbuf.at[g, dx], t_sem.at[g, dx]
        )

    def tail_remote(g, dx):
        return remote(
            tbuf.at[g, dx], a2.at[dx, pl.ds((g + 1) * tok, tok), :],
            c_snd.at[g, dx], c_rcv.at[g, dx], (partner, opposite, diagonal)[g],
        )

    def window_cols(j, width=SW):
        return pl.ds(pl.multiple_of(j * width, width), width)

    def b_load(j):
        return pltpu.make_async_copy(hid.at[0, :, window_cols(j)], hbuf.at[j], l_sem.at[j])

    def b_load_first(j):
        return pltpu.make_async_copy(emb.at[:, window_cols(j)], hbuf.at[j], l_sem.at[j])

    def b_remote(j):
        return remote(
            hbuf.at[j], b_buf.at[j, pl.ds(0, tok), :],
            b_snd.at[j], b_rcv.at[j], following,
        )

    def e_direct(j):
        return remote(
            hbuf.at[j], b2.at[j, pl.ds(0, tok), :], e_snd.at[j], e_rcv.at[j], beside
        )

    def e_relay(j):
        return remote(hbuf.at[j], relay.at[j], e_snd.at[j], k_rcv.at[j], beside)

    def e_pass(j):
        return remote(
            relay.at[j], b2.at[j, pl.ds(0, tok), :], k_snd.at[j], e_rcv.at[j], skipped
        )

    def forward(j):
        return remote(
            b_buf.at[j, pl.ds(0, tok), :], b_buf.at[j, pl.ds(tok, tok), :],
            f_snd.at[j], f_rcv.at[j], partner,
        )

    def forward2(j):
        return remote(
            b2.at[j, pl.ds(0, tok), :], b2.at[j, pl.ds(tok, tok), :],
            h_snd.at[j], h_rcv.at[j], partner,
        )

    def first(d, j, h):
        part = pl.ds(h * SW, SW)
        return remote(
            m1.at[d, j, part, :], r1.at[d, j, part, :],
            m1_snd.at[d, j, h], m1_rcv.at[d, j, h], left if d else right,
        )

    def second(d, z, j):
        return remote(
            m2.at[d, z, j], r2.at[d, z, j], m2_snd.at[d, z, j], m2_rcv.at[d, z, j],
            left if d else right,
        )

    def first2(d, u):
        return remote(
            n1.at[d, u], s1.at[d, u], n1_snd.at[d, u], n1_rcv.at[d, u], left if d else right
        )

    def second2(d, h, u):
        return remote(
            n2.at[d, h, u], s2.at[d, h, u], n2_snd.at[d, h, u], n2_rcv.at[d, h, u],
            left if d else right,
        )

    def last(j):
        return remote(zs.at[j], zr.at[j], z_snd.at[j], z_rcv.at[j], opposite)

    def factor_x(k):
        n = k - 1
        return remote(ag.at[c, zh, x], ag.at[c, zh, x], g_snd.at[n], g_rcv.at[n], (s, spot(k)))

    def factor_z():
        n = nx - 1
        return remote(ag.at[c, zh], ag.at[c, zh], g_snd.at[n], g_rcv.at[n], opposite)

    def factor_c():
        n = nx
        return remote(ag.at[c], ag.at[c], g_snd.at[n], g_rcv.at[n], partner)

    def store(j):
        return pltpu.make_async_copy(
            obuf.at[j], out.at[0, pl.ds(0, main), window_cols(j, CW)], o_sem.at[j]
        )

    def store2(j):
        return pltpu.make_async_copy(
            obuf2.at[j], out.at[0, pl.ds(main, tail), window_cols(j)], o2_sem.at[j]
        )

    def send_b(j):
        b_remote(j).start()

    def take_b(j):
        b_remote(j).wait_recv()
        forward(j).start()

    def send_b2(j):
        @pl.when(even)
        def _():
            e_direct(j).start()

        @pl.when(jnp.logical_not(even))
        def _():
            e_relay(j).start()

    def pass_b2(j):
        @pl.when(even)
        def _():
            e_relay(j).wait_recv()
            e_pass(j).start()

    def take_b2(j):
        @pl.when(even)
        def _():
            e_pass(j).wait_recv()

        @pl.when(jnp.logical_not(even))
        def _():
            e_direct(j).wait_recv()

        forward2(j).start()

    def wait_a(*pairs):
        for z, dx in pairs:
            a_local(z, dx).wait()
            a_remote(z, dx).wait_recv()

    load_counts = pltpu.make_async_copy(counts_in, counts, i_sem.at[0])
    load_owners = pltpu.make_async_copy(owners_in, owners, i_sem.at[1])
    def load_b(j, carry):
        @pl.when(s == sections - 1)
        def _():
            b_load_first(j).start()

        @pl.when(s < sections - 1)
        def _():
            b_load(j).start()

        return carry

    lax.fori_loop(0, ns, load_b, 0)
    load_counts.start()
    load_owners.start()
    for z, dx in ((0, 2), (1, 2), (1, 1), (0, 3), (0, 1), (1, 3), (0, 0), (1, 0)):
        a_local(z, dx).start()
    for dx in range(nx):
        tail_local(dx).start()
        for g in range(3):
            tail_load(g, dx).start()
    barrier = pltpu.get_barrier_semaphore()
    neighbours = (
        right, left, across, opposite, partner, diagonal, following, previous,
        beside, skipped, skipping,
    )
    for device in neighbours:
        pl.semaphore_signal(barrier, inc=1, device_id=device, device_id_type=MESH)
    ag[c, zh, x] = ainv[0, 0]
    pl.semaphore_wait(barrier, len(neighbours))

    b_load(0).wait()
    send_b(0)
    for z, dx in ((0, 2), (1, 2), (1, 1), (0, 3), (0, 1), (1, 3)):
        a_remote(z, dx).start()
    for k in range(1, nx):
        factor_x(k).start()
    send_b2(0)
    for j in range(1, EARLY):
        b_load(j).wait()
        send_b(j)
        send_b2(j)
    load_counts.wait()
    load_owners.wait()
    take_b(0)
    for z, dx in ((0, 0), (1, 0)):
        a_remote(z, dx).start()
    for j in range(EARLY, ns):
        b_load(j).wait()
        if j < AHEAD:
            send_b(j)
        send_b2(j)
    for dx in range(nx):
        tail_load(0, dx).wait()
        tail_remote(0, dx).start()

    def bounds(z, core):
        replica = spot(0, z, core)
        return counts[0, replica], counts[1, replica]

    half = tok // 2

    def transpose(source, target, j, z):
        limits = (*bounds(z, c), *bounds(z, 1 - c))
        for p in range(4):
            piece = source[j, pl.ds(p * half, half), :].astype(F32)
            slots = lax.broadcasted_iota(jnp.int32, piece.shape, 0)
            piece = jnp.where(slots < limits[p], piece, 0.0)
            target[window_cols(j), pl.ds(p * half, half)] = piece.T.astype(BF16)

    def term(j, q):
        return jnp.dot(bt[window_cols(j, CW), :], a_buf[q], preferred_element_type=F32)

    def scale(width):
        total = jnp.int32(0)
        for r in range(counts.shape[0]):
            for m in range(counts.shape[1]):
                total = total + counts[r, m]
        return 1.0 / jnp.sqrt(jnp.full((1, width), total.astype(F32)))

    def choose(t, carry):
        owner = owners[0, t]
        slot = jnp.int32(0)
        for t2 in range(window // size):
            slot = slot + jnp.where((owners[0, t2] == owner) & (t2 < t), 1, 0)
        slot = jnp.minimum(slot, ainv.shape[2] - 1)
        chosen[t] = ag[owner % 2, owner // (2 * nx), (owner // 2) % nx, slot]
        return carry

    def finish(j):
        last(j).wait_recv()
        grad = ((own[j] + zr[j].astype(F32)) * scale(main)).astype(BF16)
        adjusted = jnp.concatenate(
            [
                jnp.dot(grad[:, b * size:(b + 1) * size], ginv[0, b], preferred_element_type=F32)
                for b in range(blocks - 1)
            ],
            axis=1,
        ).astype(BF16)
        for k in range(CW // size):
            piece = jnp.dot(
                chosen[j * (CW // size) + k], adjusted[k * size:(k + 1) * size, :],
                preferred_element_type=F32,
            )
            obuf[j, :, pl.ds(k * size, size)] = piece.T.astype(BF16)
        store(j).start()

    def finish2(u, carry):
        for d in range(2):
            for h in range(2):
                second2(d, h, u).wait_recv()
        weights = scale(tail)
        grad = jnp.concatenate(
            [
                ((own2[u, h] + s2[0, h, u].astype(F32) + s2[1, h, u].astype(F32)) * weights)
                .astype(BF16)
                for h in range(2)
            ],
            axis=0,
        )
        adjusted = jnp.dot(grad, ginv[0, blocks - 1], preferred_element_type=F32).astype(BF16)
        for k in range(uw // size):
            t = u * (uw // size) + k
            piece = jnp.dot(
                chosen[t], adjusted[k * size:(k + 1) * size, :], preferred_element_type=F32
            )
            obuf2[t] = piece.T.astype(BF16)
            store2(t).start()
        return carry

    hw = uw // 2

    def begin2(u, carry):
        cols = pl.ds(pl.multiple_of(u * uw, uw), uw)
        near, far = bt[cols, :], bt2[cols, :]

        def side(start):
            return jnp.concatenate([a2[dx, pl.ds(start, 2 * tok), :] for dx in range(nx)], axis=1)

        value = jnp.dot(near, side(0), preferred_element_type=F32) + jnp.dot(
            far, side(2 * tok), preferred_element_type=F32
        )

        def block(h, dx):
            return value[h * hw:(h + 1) * hw, dx * tail:(dx + 1) * tail]

        for d in range(2):
            n1[d, u] = block(d, 2).astype(BF16)
            first2(d, u).start()
        for d, dx in ((0, 1), (1, nx - 1)):
            comb[d, u] = block(d, dx)
            n2[d, 1 - d, u] = block(1 - d, dx).astype(BF16)
        for h in range(2):
            own2[u, h] = block(h, 0)
        return carry

    def middle2(u, carry):
        for d in range(2):
            second2(d, 1 - d, u).start()
        return carry

    def end2(u, carry):
        for d in range(2):
            first2(d, u).wait_recv()
            n2[d, d, u] = (comb[d, u] + s1[d, u].astype(F32)).astype(BF16)
            second2(d, d, u).start()
        return carry

    def step(i, carry):
        @pl.when((i >= 1) & (i < nc + 1))
        def _():
            j = i - 1

            @pl.when(i == 1)
            def _():
                wait_a((0, 1), (1, 3))

            for d, q in ((0, 1), (1, nx + 3)):
                value = term(j, q)
                for h in range(SUBS):
                    first(d, j, h).wait_recv()
                m2[d, d, j] = (value + r1[d, j].astype(F32)).astype(BF16)
                second(d, d, j).start()

        @pl.when(i == 0)
        def _():
            wait_a((0, 2), (1, 2))
            for h in range(SUBS):
                if h:
                    take_b(h)
                forward(h).wait_recv()
                transpose(b_buf, bt, h, zh)
                for d, q in ((0, 2), (1, nx + 2)):
                    part = bt[pl.ds(h * SW, SW), :]
                    m1[d, 0, pl.ds(h * SW, SW), :] = jnp.dot(
                        part, a_buf[q], preferred_element_type=F32
                    ).astype(BF16)
                    first(d, 0, h).start()

        @pl.when((i > 0) & (i < nc))
        def _():
            for h in range(SUBS):
                take_b(i * SUBS + h)
            for h in range(SUBS):
                forward(i * SUBS + h).wait_recv()
                transpose(b_buf, bt, i * SUBS + h, zh)
            for d, q in ((0, 2), (1, nx + 2)):
                m1[d, i] = term(i, q).astype(BF16)
                for h in range(SUBS):
                    first(d, i, h).start()

        @pl.when(i < nc)
        def _():
            @pl.when(i == 0)
            def _():
                wait_a((1, 1), (0, 3))

            for d, q in ((0, nx + 1), (1, 3)):
                m2[d, 1 - d, i] = term(i, q).astype(BF16)
                second(d, 1 - d, i).start()

        @pl.when(i * SUBS + AHEAD < ns)
        def _():
            for h in range(SUBS):
                send_b(i * SUBS + AHEAD + h)

        pieces = [(g, dx) for g in (1, 2) for dx in range(nx)]
        for n, count in enumerate(PACE):
            @pl.when(i == n)
            def _():
                for g, dx in pieces[sum(PACE[:n]):sum(PACE[:n]) + count]:
                    tail_load(g, dx).wait()
                    tail_remote(g, dx).start()

        @pl.when(i == 1)
        def _():
            for k in range(1, nx):
                factor_x(k).wait_recv()
            factor_z().start()

        @pl.when(i == 1 + LAG)
        def _():
            factor_z().wait_recv()
            factor_c().start()

        for n, (low, high) in enumerate(PIECES2):
            @pl.when(i == n + 3)
            def _():
                for j in range(low, high):
                    forward2(j).wait_recv()
                    transpose(b2, bt2, j, 1 - zh)

        @pl.when(i == nc)
        def _():
            for dx in range(nx):
                tail_local(dx).wait()
                for g in range(3):
                    tail_remote(g, dx).wait_recv()
            lax.fori_loop(0, nu, begin2, 0)
            lax.fori_loop(0, nu, middle2, 0)

        @pl.when(i >= 2)
        def _():
            j = i - 2

            @pl.when(i == 2)
            def _():
                wait_a((0, 0), (1, 0))

            away = term(j, (1 - zh) * nx)
            second(0, 1, j).wait_recv()
            second(1, 0, j).wait_recv()
            second(0, 0, j).wait_recv()
            second(1, 1, j).wait_recv()
            zs[j] = (
                away + r2[0, 1 - zh, j].astype(F32) + r2[1, 1 - zh, j].astype(F32)
            ).astype(BF16)
            last(j).start()
            mine = term(j, zh * nx)
            own[j] = mine + r2[0, zh, j].astype(F32) + r2[1, zh, j].astype(F32)

        @pl.when(i == nc + 1)
        def _():
            lax.fori_loop(0, nu, end2, 0)

        for n, (low, high) in enumerate(PIECES2):
            @pl.when(i == n + 1)
            def _():
                for j in range(low, high):
                    pass_b2(j)

            @pl.when(i == n + 2)
            def _():
                for j in range(low, high):
                    take_b2(j)

        @pl.when(i == 2 + LAG)
        def _():
            factor_c().wait_recv()
            lax.fori_loop(0, window // size, choose, 0)

        @pl.when(i >= 2 + LAG)
        def _():
            finish(i - 2 - LAG)

        return carry

    lax.fori_loop(0, nc + 2, step, 0)

    def drain(j, carry):
        b_remote(j).wait_send()

        @pl.when(even)
        def _():
            e_direct(j).wait_send()
            e_pass(j).wait_send()

        @pl.when(jnp.logical_not(even))
        def _():
            e_relay(j).wait_send()

        forward(j).wait_send()
        forward2(j).wait_send()
        return carry

    def drain1(j, carry):
        for d in range(2):
            for h in range(SUBS):
                first(d, j, h).wait_send()
            for z in range(2):
                second(d, z, j).wait_send()
        return carry

    def drain2(u, carry):
        for d in range(2):
            first2(d, u).wait_send()
            for h in range(2):
                second2(d, h, u).wait_send()
        return carry

    def drain3(j, carry):
        last(j).wait_send()
        store(j).wait()
        for h in range(SUBS):
            store2(j * SUBS + h).wait()
        return carry

    def rest(j, carry):
        finish(j)
        return carry

    lax.fori_loop(nc - LAG, nc - 1, rest, 0)
    for dx in range(nx):
        for z in range(2):
            a_remote(z, dx).wait_send()
        for g in range(3):
            tail_remote(g, dx).wait_send()
    for k in range(1, nx):
        factor_x(k).wait_send()
    factor_z().wait_send()
    factor_c().wait_send()
    lax.fori_loop(0, ns, drain, 0)
    lax.fori_loop(0, nc, drain1, 0)
    finish(nc - 1)
    lax.fori_loop(0, nu, finish2, 0)
    lax.fori_loop(0, nu, drain2, 0)
    lax.fori_loop(0, nc, drain3, 0)


def local(sections, groups, embedded, hidden_out, out_grads, counts, owners, ginv, ainv):
    tok, window = embedded.shape
    rows = out_grads.shape[-1] // groups
    size = ginv.shape[-1]
    main = rows - size
    nx = groups // 4
    nc, ns, nu = window // CW, window // SW, window // UW
    hw = UW // 2
    dims = (sections, nx, rows, tok, window)
    hbm = pl.BlockSpec(memory_space=pl.ANY)
    vmem = pl.BlockSpec(memory_space=pltpu.VMEM)
    dma = pltpu.SemaphoreType.DMA
    flops = 2 * tok * out_grads.shape[-1] * window
    return pl.pallas_call(
        functools.partial(kernel, dims),
        out_shape=jax.ShapeDtypeStruct((1, rows, window), BF16),
        in_specs=[hbm, hbm, hbm, hbm, hbm, vmem, vmem],
        out_specs=hbm,
        scratch_shapes=[
            pltpu.SMEM(counts.shape[::-1], jnp.int32),
            pltpu.SMEM(owners.shape[:2], jnp.int32),
            pltpu.VMEM((2 * nx, 2 * tok, main), BF16),
            pltpu.VMEM((nx, 4 * tok, size), BF16),
            pltpu.VMEM((ns, 2 * tok, SW), BF16),
            pltpu.VMEM((ns, 2 * tok, SW), BF16),
            pltpu.VMEM((window, 2 * tok), BF16),
            pltpu.VMEM((window, 2 * tok), BF16),
            pltpu.VMEM((2, nc, CW, main), BF16),
            pltpu.VMEM((2, nc, CW, main), BF16),
            pltpu.VMEM((2, 2, nc, CW, main), BF16),
            pltpu.VMEM((2, 2, nc, CW, main), BF16),
            pltpu.VMEM((nc, CW, main), F32),
            pltpu.VMEM((nc, CW, main), BF16),
            pltpu.VMEM((nc, CW, main), BF16),
            pltpu.VMEM((2, nu, hw, size), BF16),
            pltpu.VMEM((2, nu, hw, size), BF16),
            pltpu.VMEM((2, 2, nu, hw, size), BF16),
            pltpu.VMEM((2, 2, nu, hw, size), BF16),
            pltpu.VMEM((2, nu, hw, size), F32),
            pltpu.VMEM((nu, 2, hw, size), F32),
            pltpu.VMEM((2, 2, nx) + ainv.shape[2:], BF16),
            pltpu.VMEM((window // size, size, size), BF16),
            pltpu.VMEM((nc, main, CW), BF16),
            pltpu.VMEM((ns, size, SW), BF16),
            pltpu.VMEM((ns, tok, SW), BF16),
            pltpu.VMEM((3, nx, tok, size), BF16),
            pltpu.VMEM((ns, tok, SW), BF16),
            dma((2,)), dma((ns,)), dma((3, nx)), dma((ns,)), dma((ns,)), dma((2 * nx,)), dma((2 * nx,)), dma((2 * nx,)),
            dma((nx,)), dma((3, nx)), dma((3, nx)),
            dma((ns,)), dma((ns,)), dma((ns,)), dma((ns,)), dma((ns,)), dma((ns,)),
            dma((ns,)), dma((ns,)),
            dma((2, nc, SUBS)), dma((2, nc, SUBS)), dma((2, 2, nc)), dma((2, 2, nc)),
            dma((2, nu)), dma((2, nu)), dma((2, 2, nu)), dma((2, 2, nu)),
            dma((nc,)), dma((nc,)), dma((nx + 1,)), dma((nx + 1,)), dma((nc,)), dma((ns,)),
        ],
        compiler_params=pltpu.CompilerParams(
            collective_id=0, has_side_effects=True, vmem_limit_bytes=60 << 20
        ),
        cost_estimate=pl.CostEstimate(
            flops=flops, bytes_accessed=2 * out_grads.size, transcendentals=0
        ),
    )(embedded, hidden_out, out_grads, counts.T, owners[:, :, 0], ginv, ainv)


def solution(mesh):
    placed = (
        P("dp", None),
        P("section", "dp", None),
        P("section", "dp", None),
        P(),
        P("section", None, None),
        P("section", "dp", None, None),
        P("section", "dp", None, None, None),
    )
    return jax.shard_map(
        functools.partial(local, mesh.shape["section"], mesh.shape["dp"]),
        mesh=mesh, in_specs=placed, out_specs=P("section", "dp", None), check_vma=False,
    )
```
